128 devices in a mesh: tower: 2 (over x_lo), dp: 64 (over x_hi, z, y, core).
Axes of the slice: x: 4 (x_hi: 2, x_lo: 2; x = x_hi * 2 + x_lo), y: 4, z: 4, core: 2. Of those that a mesh axis runs over, the one named last changes fastest.
Arguments:
- token_states: bfloat16 [2, 1024, 64, 768], P('tower', 'dp'), may hold values from -8 to 8
- qkv_weight: bfloat16 [2, 1, 768, 2304], P('tower'), may hold values from -0.21875 to 0.21875
- out_weight: bfloat16 [2, 1, 768, 768], P('tower'), may hold values from -0.21875 to 0.21875
- up_weight: bfloat16 [2, 1, 768, 3072], P('tower'), may hold values from -0.21875 to 0.21875
- down_weight: bfloat16 [2, 1, 3072, 768], P('tower'), may hold values from -0.109375 to 0.109375
- queue_states: bfloat16 [65536, 768], P(('tower', 'dp')), may hold values from -16 to 16
- queue_ids: int32 [65536], P(('tower', 'dp')), may hold values from 0 to 7
- positive: int32 [1024], replicated, may hold values from 0 to 1023, as said below
- tail_ids: int32 [1024], replicated, may hold values from 0 to 7
Outputs:
- query_loss: float32 [1024], P('dp')
- query_grad: float32 [1024, 768], P(('tower', 'dp'))
- tail_grad: float32 [1024, 768], P('dp')
The draws below stay inside these ranges and needn't reach their ends.
Inputs may be any that keep to these rules, and one draw needn't show every extreme that they name: Each of the 1024 tails is the positive of exactly one query.
All inputs are finite; a program needn't handle non-finite values.
Results may differ from the reference program's by a relative error of at most 0.02.
Values may be sent and summed in bfloat16 or wider, within the bound.
A program may use at most 128 MiB of HBM per device.

```python
import math
import jax
import jax.numpy as jnp
from jax import lax

D = 768
HEADS = 12
FF = 3072
SEQ = 64
LAYERS = 1
HEAD_DIM = 64
BATCH = 1024
QUEUE = 65536


cluster_total = 64


def cluster_layout(key):
    tail_order = jax.random.permutation(jax.random.fold_in(key, 701), BATCH).astype(jnp.int32)
    query_group = jax.random.randint(jax.random.fold_in(key, 702), (BATCH,), 0, cluster_total, dtype=jnp.int32)
    tail_group = jnp.zeros((BATCH,), jnp.int32).at[tail_order].set(query_group)
    queue_group = jax.random.randint(jax.random.fold_in(key, 703), (QUEUE,), 0, cluster_total, dtype=jnp.int32)
    return (tail_order, query_group, tail_group, queue_group)


def cluster_centres(key):
    return jax.random.normal(jax.random.fold_in(key, 704), (cluster_total, D), jnp.float32)


def draw_token_states(key, part):
    tail_order, query_group, tail_group, queue_group = cluster_layout(key)
    centres = cluster_centres(key)
    key = jax.random.fold_in(key, 11)
    centre_rows = centres[jnp.stack([query_group, tail_group])][:, :, None, :]
    jitter = jax.random.normal(key, (2, BATCH, SEQ, D), jnp.float32)
    values = centre_rows + jitter
    return jnp.clip(values, -8.0, 8.0).astype(jnp.bfloat16)


def draw_queue_states(key, part):
    tail_order, query_group, tail_group, queue_group = cluster_layout(key)
    centres = cluster_centres(key)
    key = jax.random.fold_in(key, 12)
    centre_rows = centres[queue_group]
    jitter = jax.random.normal(jax.random.fold_in(key, 1), (QUEUE, D), jnp.float32)
    values = centre_rows + 0.8 * jitter
    return jnp.clip(values, -16.0, 16.0).astype(jnp.bfloat16)


def draw_positive(key, part):
    tail_order, query_group, tail_group, queue_group = cluster_layout(key)
    return tail_order


def with_ends(drawn, rng, smallest, high):
    longest = drawn.shape.index(max(drawn.shape))
    spots = []
    for shift in (0, 1):
        where = [jax.random.randint(jax.random.fold_in(rng, axis), (), 0, length) for axis, length in enumerate(drawn.shape)]
        where[longest] = (where[longest] + shift) % drawn.shape[longest]
        spots.append(tuple(where))
    return drawn.at[spots[0]].set(smallest).at[spots[1]].set(high)


def level_of(stream_key, dims, pieces, least, top_value):
    def one(axis_at, parts):
        draws = jax.random.uniform(jax.random.fold_in(jax.random.fold_in(stream_key, 6), axis_at), (parts,), jnp.float32, least / len(pieces), top_value / len(pieces))
        return jnp.repeat(jnp.exp(draws), dims[axis_at] // parts).reshape((-1,) + (1,) * (len(dims) - axis_at - 1))

    loudness = one(*pieces[0])
    for cut in pieces[1:]:
        loudness = loudness * one(*cut)
    return loudness


def noise(stream_key, dims, scale, most, shards=(), kind=jnp.bfloat16):
    values = jax.random.normal(stream_key, dims, jnp.float32) * scale
    if len(shards) > 0:
        values = level_of(stream_key, dims, shards, -0.22, 0.18) * values
    return jnp.clip(values, min=-most, max=most).astype(kind)


def setup_inputs(seed: int = 0) -> dict:
    keys = jax.random.split(jax.random.key(seed), 10)
    return {
        "token_states": draw_token_states(jax.random.fold_in(keys[9], 71), 0),
        "qkv_weight": noise(keys[1], (2, LAYERS, D, 3 * D), D ** -0.5, 0.21875, ((0, 2),)),
        "out_weight": noise(keys[2], (2, LAYERS, D, D), D ** -0.5, 0.21875, ((0, 2),)),
        "up_weight": noise(keys[3], (2, LAYERS, D, FF), D ** -0.5, 0.21875, ((0, 2),)),
        "down_weight": noise(keys[4], (2, LAYERS, FF, D), FF ** -0.5, 0.109375, ((0, 2),)),
        "queue_states": draw_queue_states(jax.random.fold_in(keys[9], 71), 0),
        "queue_ids": with_ends(jax.random.randint(keys[6], (QUEUE,), 0, 8), jax.random.fold_in(keys[6], 1), 0, 7).astype(jnp.int32),
        "positive": draw_positive(jax.random.fold_in(keys[9], 71), 0),
        "tail_ids": with_ends(jax.random.randint(keys[8], (BATCH,), 0, 8), jax.random.fold_in(keys[8], 1), 0, 7).astype(jnp.int32),
    }


EPS_NORM = 1e-05
EPS_UNIT = 1e-06
INV_TEMP = 50.0
MARGIN = 1.0

def norm_rows(values):
    average = lax.optimization_barrier(jnp.mean(values, axis=-1, keepdims=True))
    centered = values - average
    spread = lax.optimization_barrier(jnp.mean(centered * centered, axis=-1, keepdims=True))
    return centered / jnp.sqrt(spread + EPS_NORM)

def unit_rows(values):
    return (values / jnp.sqrt(lax.optimization_barrier(jnp.sum(values * values, axis=-1, keepdims=True)) + EPS_UNIT)).astype(jnp.bfloat16)

def encoder_layer(hidden, qkv_w, out_w, up_w, down_w):
    text_count, length, model_width = hidden.shape
    flat_in = hidden.reshape(text_count * length, model_width)
    qkv_all = jnp.dot(flat_in, qkv_w, preferred_element_type=jnp.float32).astype(jnp.bfloat16)
    qkv_all = qkv_all.reshape(text_count, length, 3, HEADS, HEAD_DIM)
    query_part = qkv_all[:, :, 0].astype(jnp.float32)
    key_part = qkv_all[:, :, 1].astype(jnp.float32)
    value_part = qkv_all[:, :, 2].astype(jnp.float32)
    scores = jnp.einsum('rshd,rthd->rhst', query_part, key_part) * (1.0 / math.sqrt(HEAD_DIM))
    exp_scores = jnp.exp(scores)
    weights_bf = (exp_scores / lax.optimization_barrier(jnp.sum(exp_scores, axis=-1, keepdims=True))).astype(jnp.bfloat16)
    context = jnp.einsum('rhst,rthd->rshd', weights_bf.astype(jnp.float32), value_part).astype(jnp.bfloat16)
    context = context.reshape(text_count * length, model_width)
    attended = jnp.dot(context, out_w, preferred_element_type=jnp.float32)
    normed = norm_rows(flat_in.astype(jnp.float32) + attended).astype(jnp.bfloat16)
    hidden_act = jax.nn.gelu(jnp.dot(normed, up_w, preferred_element_type=jnp.float32), approximate=False).astype(jnp.bfloat16)
    result = norm_rows(normed.astype(jnp.float32) + jnp.dot(hidden_act, down_w, preferred_element_type=jnp.float32))
    return result.astype(jnp.bfloat16).reshape(text_count, length, model_width)

def encode(states, qkv_w, out_w, up_w, down_w):
    hidden = states
    for layer_idx in range(LAYERS):
        hidden = encoder_layer(hidden, qkv_w[layer_idx], out_w[layer_idx], up_w[layer_idx], down_w[layer_idx])
    pooled = lax.optimization_barrier(jnp.mean(hidden.astype(jnp.float32), axis=1))
    return unit_rows(pooled)

def reference(token_states, qkv_weight, out_weight, up_weight, down_weight, queue_states, queue_ids, positive, tail_ids):
    query_emb = encode(token_states[0], qkv_weight[0], out_weight[0], up_weight[0], down_weight[0])
    tail_emb = encode(token_states[1], qkv_weight[1], out_weight[1], up_weight[1], down_weight[1])
    queue_keys = unit_rows(queue_states.astype(jnp.float32))
    tail_index = jnp.arange(BATCH, dtype=jnp.int32)
    pos_mask = positive[:, None] == tail_index[None, :]
    true_ids = tail_ids[positive]
    tail_scores = INV_TEMP * jnp.dot(query_emb, tail_emb.T, preferred_element_type=jnp.float32) - MARGIN * pos_mask.astype(jnp.float32)
    kept_mask = pos_mask | (tail_ids[None, :] != true_ids[:, None])
    tail_exp = jnp.where(kept_mask, jnp.exp(tail_scores), jnp.float32(0.0))
    queue_scores = INV_TEMP * jnp.dot(query_emb, queue_keys.T, preferred_element_type=jnp.float32)
    queue_exp = jnp.where(queue_ids[None, :] != true_ids[:, None], jnp.exp(queue_scores), jnp.float32(0.0))
    row_total = lax.optimization_barrier(jnp.sum(tail_exp, axis=1)) + lax.optimization_barrier(jnp.sum(queue_exp, axis=1))
    pos_logit = lax.optimization_barrier(jnp.sum(jnp.where(pos_mask, tail_scores, jnp.float32(0.0)), axis=1))
    query_loss = jnp.log(row_total) - pos_logit
    tail_weights = (tail_exp / row_total[:, None] - pos_mask.astype(jnp.float32)).astype(jnp.bfloat16)
    queue_weights = (queue_exp / row_total[:, None]).astype(jnp.bfloat16)
    query_grad = INV_TEMP * (jnp.dot(tail_weights, tail_emb, preferred_element_type=jnp.float32) + jnp.dot(queue_weights, queue_keys, preferred_element_type=jnp.float32))
    tail_grad = INV_TEMP * jnp.dot(tail_weights.T, query_emb, preferred_element_type=jnp.float32)
    return (query_loss, query_grad, tail_grad)
```

```python
import functools
import jax, jax.numpy as jnp
from jax import lax
from jax.experimental import pallas as pl
from jax.experimental.pallas import tpu as pltpu
from jax.sharding import PartitionSpec as P

BF = jnp.bfloat16
F32 = jnp.float32
SEQ = 64

def dot(a, b):
    return jnp.dot(a, b, preferred_element_type=F32)

def dot_t(a, b):
    return lax.dot_general(a, b, (((1,), (1,)), ((), ())), preferred_element_type=F32)

def gelu(x, kind="as"):
    if kind == "none":
        return jnp.maximum(x, 0.0)
    if kind == "erf":
        return 0.5 * x * (1.0 + lax.erf(x * 0.7071067811865476))
    a = jnp.abs(x)
    t = pl.reciprocal(1.0 + (0.3275911 * 0.7071067811865476) * a, approx=True)
    p = 0.5 * 1.061405429
    for c in (-1.453152027, 1.421413741, -0.284496736, 0.254829592):
        p = p * t + 0.5 * c
    q = p * t * jnp.exp2((x * x) * (-0.5 * 1.4426950408889634))
    return jnp.maximum(x, 0.0) - a * q

def norm_rows(v):
    avg = jnp.mean(v, axis=-1, keepdims=True)
    c = v - avg
    s = jnp.mean(c * c, axis=-1, keepdims=True)
    return c * lax.rsqrt(s + 1e-5)

def unit_rows(v):
    return v * lax.rsqrt(jnp.sum(v * v, axis=-1, keepdims=True) + 1e-6)

def enc_chunk(x, wqkv, wout, wup, wdown, waits, kind="as", fft=768, attn=True):
    m = x.shape[0]
    nt = m // SEQ
    waits[0]()
    row = lax.broadcasted_iota(jnp.int32, (256, 256), 0) // SEQ
    col = lax.broadcasted_iota(jnp.int32, (256, 256), 1) // SEQ
    ones_bd = jnp.where(row == col, 1.0, 0.0).astype(BF)
    ctx = []
    if attn:
        lane = lax.broadcasted_iota(jnp.int32, (SEQ, 128), 1)
        low = lane < 64
        zero = jnp.zeros((SEQ, 128), BF)
        def bd(t):
            a, b = t[:, :128], t[:, 128:]
            z = jnp.zeros_like(a)
            rows = [
                jnp.concatenate([jnp.where(low, a, z), zero], 1),
                jnp.concatenate([jnp.where(low, z, a), zero], 1),
                jnp.concatenate([zero, jnp.where(low, b, z)], 1),
                jnp.concatenate([zero, jnp.where(low, z, b)], 1),
            ]
            return jnp.concatenate(rows, 0)
        for g in range(3):
            q = (dot(x, wqkv[:, g * 256:(g + 1) * 256])).astype(BF) * BF(0.125)
            k = (dot(x, wqkv[:, 768 + g * 256:768 + (g + 1) * 256])).astype(BF)
            v = (dot(x, wqkv[:, 1536 + g * 256:1536 + (g + 1) * 256])).astype(BF)
            es = []
            for t in range(nt):
                sl = slice(t * SEQ, (t + 1) * SEQ)
                es.append(jnp.exp(dot_t(q[sl], bd(k[sl]))))
            e = jnp.concatenate(es, 0)
            p = (e / dot(e.astype(BF), ones_bd)).astype(BF)
            cs = []
            for t in range(nt):
                sl = slice(t * SEQ, (t + 1) * SEQ)
                cs.append(dot(p[sl], bd(v[sl])).astype(BF))
            ctx.append(jnp.concatenate(cs, 0))
        ctx = jnp.concatenate(ctx, 1)
    else:
        qkv = dot(x, wqkv[...]).astype(BF)
        ctx = qkv[:, :768] + qkv[:, 768:1536] + qkv[:, 1536:]
    waits[1]()
    normed = norm_rows(x.astype(F32) + dot(ctx, wout[...])).astype(BF)
    waits[2]()
    acc = normed.astype(F32)
    for j in range(0, 3072, fft):
        act = gelu(dot(normed, wup[:, j:j + fft]), kind).astype(BF)
        if j == 0:
            waits[3]()
        acc = acc + dot(act, wdown[j:j + fft, :])
    hid = norm_rows(acc).astype(BF).astype(F32)
    pooled = jnp.mean(hid.reshape(nt, SEQ, 768), axis=1)
    return unit_rows(pooled)

def enc_kernel(x_ref, qkv_h, out_h, up_h, down_h, o_ref, wqkv, wout, wup, wdown, sems, *, kind, fft, attn):
    step = pl.program_id(0)
    cps = [pltpu.make_async_copy(s.at[0, 0], d, sems.at[i]) for i, (s, d) in enumerate(
        [(qkv_h, wqkv), (out_h, wout), (up_h, wup), (down_h, wdown)])]
    @pl.when(step == 0)
    def _():
        for c in cps:
            c.start()
    def waiter(c):
        def f():
            @pl.when(step == 0)
            def _():
                c.wait()
        return f
    emb = enc_chunk(x_ref[0], wqkv, wout, wup, wdown, [waiter(c) for c in cps], kind, fft, attn)
    o_ref[0] = emb

def encode(x, qkv, out, up, down, m=512, kind="as", fft=768, attn=True):
    n = 1024 // m
    x = x.reshape(n, m, 768)
    return pl.pallas_call(
        functools.partial(enc_kernel, kind=kind, fft=fft, attn=attn),
        grid=(n,),
        out_shape=jax.ShapeDtypeStruct((n, m // SEQ, 768), F32),
        in_specs=[pl.BlockSpec((1, m, 768), lambda i: (i, 0, 0))] + [pl.BlockSpec(memory_space=pl.ANY)] * 4,
        out_specs=pl.BlockSpec((1, m // SEQ, 768), lambda i: (i, 0, 0)),
        scratch_shapes=[pltpu.VMEM((768, 2304), BF), pltpu.VMEM((768, 768), BF), pltpu.VMEM((768, 3072), BF),
                        pltpu.VMEM((3072, 768), BF), pltpu.SemaphoreType.DMA((4,))],
        compiler_params=pltpu.CompilerParams(vmem_limit_bytes=60 * 2**20),
    )(x, qkv, out, up, down)


MESH = pl.DeviceIdType.MESH
INV_TEMP = 50.0


def coords():
    t, dp = lax.axis_index("tower"), lax.axis_index("dp")
    core = lax.rem(dp, 2)
    y = lax.rem(lax.div(dp, 2), 4)
    z = lax.rem(lax.div(dp, 8), 4)
    x = lax.div(dp, 32) * 2 + t
    return core, (y, z, x)


def device_of(core, at):
    y, z, x = at
    return (lax.rem(x, 2), ((lax.div(x, 2) * 4 + z) * 4 + y) * 2 + core)


def moved(at, axis, step):
    return tuple(lax.rem(v + step, 4) if i == axis else v for i, v in enumerate(at))


def transpose_col(col):
    n = col.shape[0]
    return jnp.transpose(jnp.broadcast_to(col, (n, 128)))[0:1, :]


def contrast_kernel(
    emb_ref, queue_ref, qid_ref, pos_ref, tid_ref,
    loss_ref, qgrad_ref, tgrad_ref,
    gath, queries, tails, keys, parts, part_c, sum_a, part_a, sum_b, part_b, sum_d, part_d,
    tot, tot_c, tot_in,
    ag_send, ag_recv, fw_send, fw_recv, c_send, c_recv, rs_send, rs_recv, t_send, t_recv,
):
    core, at = coords()
    mate = 1 - core
    mate_dev = device_of(mate, at)
    tower, dp = lax.axis_index("tower"), lax.axis_index("dp")
    peers = [device_of(core, moved(at, axis, step)) for axis in range(3) for step in (1, 2, 3)]

    barrier = pltpu.get_barrier_semaphore()
    for dev in peers + [mate_dev]:
        pl.semaphore_signal(barrier, inc=1, device_id=dev, device_id_type=MESH)

    sends = []

    def send(src, dst, ssem, rsem, dev):
        c = pltpu.make_async_remote_copy(src_ref=src, dst_ref=dst, send_sem=ssem, recv_sem=rsem, device_id=dev, device_id_type=MESH)
        c.start()
        sends.append(c)

    def arrive(dst, ssem, rsem):
        pltpu.make_async_remote_copy(src_ref=dst, dst_ref=dst, send_sem=ssem, recv_sem=rsem, device_id=mate_dev, device_id_type=MESH).wait_recv()

    order = [[k, (k + 1) % 3, (k + 2) % 3] for k in range(3)]
    idx = [[at[a] for a in order[k]] for k in range(3)]

    for k in range(3):
        gath[k, core, idx[k][2], idx[k][1], idx[k][0]] = emb_ref[:, k * 256:(k + 1) * 256].astype(BF)

    pl.semaphore_wait(barrier, 10)

    def piece(k, stage, who, step):
        i0, i1, i2 = idx[k]
        if stage == 0:
            return gath.at[k, who, i2, i1, lax.rem(i0 + step, 4)]
        if stage == 1:
            return gath.at[k, who, i2, lax.rem(i1 + step, 4)]
        return gath.at[k, who, lax.rem(i2 + step, 4)]

    for stage in range(3):
        for k in range(3):
            src = piece(k, stage, core, 0)
            for step in (1, 2, 3):
                send(src, src, ag_send.at[k, stage, step - 1], ag_recv.at[k, stage, step - 1],
                     device_of(core, moved(at, order[k][stage], step)))
            if stage > 0:
                if stage == 1:
                    send(src, src, fw_send.at[k, 0], fw_recv.at[k, 0], mate_dev)
                else:
                    for step in (1, 2, 3):
                        p = piece(k, 1, core, step)
                        send(p, p, fw_send.at[k, step], fw_recv.at[k, step], mate_dev)
        if stage == 0:
            def key_rows(i, _):
                rows = pl.ds(pl.multiple_of(i * 128, 128), 128)
                keys[rows, :] = unit_rows(queue_ref[rows, :].astype(F32)).astype(BF)
                return 0
            lax.fori_loop(0, 4, key_rows, 0)
        for k in range(3):
            for step in (1, 2, 3):
                arrive(piece(k, stage, core, 4 - step), ag_send.at[k, stage, step - 1], ag_recv.at[k, stage, step - 1])
                if stage == 2:
                    p = piece(k, 2, core, 4 - step)
                    send(p, p, fw_send.at[k, 3 + step], fw_recv.at[k, 3 + step], mate_dev)
    for k in range(3):
        arrive(piece(k, 1, mate, 0), fw_send.at[k, 0], fw_recv.at[k, 0])
        for step in (1, 2, 3):
            p = piece(k, 1, mate, step)
            arrive(p, fw_send.at[k, step], fw_recv.at[k, step])
            p = piece(k, 2, mate, 4 - step)
            arrive(p, fw_send.at[k, 3 + step], fw_recv.at[k, 3 + step])

    def assemble(n, _):
        y, z, xh = lax.rem(n, 4), lax.rem(lax.div(n, 4), 4), lax.div(n, 16)
        for who in range(2):
            rows = pl.ds(pl.multiple_of(n * 32 + who * 16, 16), 16)
            for side, dst in ((0, queries), (1, tails)):
                place = (y, z, 2 * xh + side)
                for k in range(3):
                    j0, j1, j2 = (place[a] for a in order[k])
                    dst[rows, k * 256:(k + 1) * 256] = gath[k, who, j2, j1, j0]
        return 0

    lax.fori_loop(0, 32, assemble, 0)

    pos = pos_ref[...]
    tid = tid_ref[...].astype(F32)
    true_row = jnp.zeros((1, 1024), F32)
    for j in range(0, 1024, 256):
        hot = (lax.broadcasted_iota(jnp.int32, (256, 1024), 0) + j == pos).astype(F32).astype(BF)
        true_row = true_row + dot(jnp.broadcast_to(tid[:, j:j + 256], (16, 256)).astype(BF), hot)[0:1, :]
    true_col = jnp.transpose(jnp.broadcast_to(true_row, (128, 1024)))[:, 0:1]
    qid = qid_ref[...].astype(F32)

    base = dp * 16
    own_tails = tails[pl.ds(pl.multiple_of(base, 16), 16), :]
    all_queries = queries[...]
    lane = lax.broadcasted_iota(jnp.int32, (16, 1024), 1)
    row = lax.broadcasted_iota(jnp.int32, (16, 1024), 0)
    own_ids = jnp.sum(jnp.where(lane == base + row, tid, 0.0), axis=1, keepdims=True)
    is_pos = pos == base + row
    tail_scores = INV_TEMP * dot_t(own_tails, all_queries) - is_pos.astype(F32)
    tail_exp = jnp.where(is_pos | (own_ids != true_row), jnp.exp(tail_scores), 0.0)
    side = jnp.where(tower == 0, 1.0, 0.0).astype(F32)
    negative = (jnp.where(is_pos, 0.0, tail_exp) * side)
    tot_row = jnp.sum(tail_exp, axis=0, keepdims=True) * side
    key_rows_bf = keys[...]
    queue_rows = []
    for xc in range(4):
        rows = slice(xc * 256, (xc + 1) * 256)
        x_at = 2 * (xc % 2) + xc // 2
        s = INV_TEMP * dot_t(all_queries[rows], key_rows_bf)
        e = jnp.where(true_col[rows] != qid, jnp.exp(s), 0.0)
        queue_rows.append(transpose_col(jnp.sum(e, axis=1, keepdims=True)))
        neg = jnp.transpose(negative[:, rows])
        u = dot(e.astype(BF), key_rows_bf) + dot(neg.astype(BF), own_tails)
        u = u.reshape(4, 4, 2, 8, 768)
        for z in range(4):
            for y in range(4):
                for who in range(2):
                    place = (y, z, x_at)
                    for k in range(3):
                        j0, j1, j2 = (place[a] for a in order[k])
                        blk = jnp.concatenate([u[z, y, who, :, k * 256:k * 256 + 128], u[z, y, who, :, k * 256 + 128:k * 256 + 256]], axis=0)
                        parts[k, who, j2, j1, j0] = blk.astype(BF)
    tot[0] = tot_row + jnp.concatenate(queue_rows, axis=1)

    for k in range(3):
        send(parts.at[k, mate], part_c.at[k], c_send.at[k], c_recv.at[k], mate_dev)
    send(tot.at[0], tot_c, t_send.at[0, 0], t_recv.at[0, 0], mate_dev)

    lane = lax.broadcasted_iota(jnp.int32, (32, 1024), 1)
    row = lax.broadcasted_iota(jnp.int32, (32, 1024), 0)
    start = tower * 512 + dp * 8
    want = jnp.where(row < 16, start + row, base + row - 16)
    sel = lane == want
    own_q = dot(sel.astype(F32).astype(BF), all_queries)
    own_pos = jnp.sum(jnp.where(sel, pos.astype(F32), 0.0), axis=1, keepdims=True).astype(jnp.int32)
    pos_emb = dot((lane == own_pos).astype(F32).astype(BF), tails[...])
    logit = INV_TEMP * jnp.sum(own_q * pos_emb, axis=1, keepdims=True) - 1.0

    arrive(tot_c, t_send.at[0, 0], t_recv.at[0, 0])
    total = tot[0] + tot_c[...]
    for axis in range(3):
        tot[axis + 1] = total
        for step in (1, 2, 3):
            send(tot.at[axis + 1], tot_in.at[axis, step - 1], t_send.at[axis + 1, step - 1], t_recv.at[axis + 1, step - 1],
                 device_of(core, moved(at, axis, step)))
        if axis == 0:
            for k in range(3):
                arrive(part_c.at[k], c_send.at[k], c_recv.at[k])
                sum_a[k] = (parts[k, core].astype(F32) + part_c[k].astype(F32)).astype(BF)
                i2 = idx[k][2]
                for step in (1, 2, 3):
                    send(sum_a.at[k, lax.rem(i2 + step, 4)], part_a.at[k, step - 1], rs_send.at[k, 0, step - 1], rs_recv.at[k, 0, step - 1],
                         device_of(core, moved(at, order[k][2], step)))
        elif axis == 1:
            for k in range(3):
                for step in (1, 2, 3):
                    arrive(part_a.at[k, step - 1], rs_send.at[k, 0, step - 1], rs_recv.at[k, 0, step - 1])
                acc = sum_a[k, idx[k][2]].astype(F32)
                for step in range(3):
                    acc = acc + part_a[k, step].astype(F32)
                sum_b[k] = acc.astype(BF)
                for step in (1, 2, 3):
                    send(sum_b.at[k, lax.rem(idx[k][1] + step, 4)], part_b.at[k, step - 1], rs_send.at[k, 1, step - 1], rs_recv.at[k, 1, step - 1],
                         device_of(core, moved(at, order[k][1], step)))
        else:
            for k in range(3):
                for step in (1, 2, 3):
                    arrive(part_b.at[k, step - 1], rs_send.at[k, 1, step - 1], rs_recv.at[k, 1, step - 1])
                acc = sum_b[k, idx[k][1]].astype(F32)
                for step in range(3):
                    acc = acc + part_b[k, step].astype(F32)
                sum_d[k] = acc.astype(BF)
                for step in (1, 2, 3):
                    send(sum_d.at[k, lax.rem(idx[k][0] + step, 4)], part_d.at[k, step - 1], rs_send.at[k, 2, step - 1], rs_recv.at[k, 2, step - 1],
                         device_of(core, moved(at, order[k][0], step)))
        for step in (1, 2, 3):
            arrive(tot_in.at[axis, step - 1], t_send.at[axis + 1, step - 1], t_recv.at[axis + 1, step - 1])
        total = total + tot_in[axis, 0] + tot_in[axis, 1] + tot_in[axis, 2]

    weights = (tail_exp / total - is_pos.astype(F32)).astype(BF)
    tgrad_ref[...] = INV_TEMP * dot(weights, all_queries)
    own_total = jnp.sum(jnp.where(sel, total, 0.0), axis=1, keepdims=True)
    loss = jnp.log(own_total[16:]) - logit[16:]
    eye = lax.broadcasted_iota(jnp.int32, (16, 16), 0) == lax.broadcasted_iota(jnp.int32, (16, 16), 1)
    loss_ref[...] = jnp.sum(jnp.where(eye, loss, 0.0), axis=0, keepdims=True)
    excess = jnp.exp(logit[:8]) / own_total[:8] - 1.0
    cols = []
    for k in range(3):
        for step in (1, 2, 3):
            arrive(part_d.at[k, step - 1], rs_send.at[k, 2, step - 1], rs_recv.at[k, 2, step - 1])
        acc = sum_d[k, idx[k][0]].astype(F32)
        for step in range(3):
            acc = acc + part_d[k, step].astype(F32)
        cols += [acc[:8], acc[8:]]
    u = jnp.concatenate(cols, axis=1)
    qgrad_ref[...] = INV_TEMP * (u / own_total[:8] + excess * pos_emb[:8])
    for c in sends:
        c.wait_send()


def contrast(emb, queue_states, queue_ids, positive, tail_ids):
    vm = pl.BlockSpec(memory_space=pltpu.VMEM)
    dma = pltpu.SemaphoreType.DMA
    loss, qgrad, tgrad = pl.pallas_call(
        contrast_kernel,
        out_shape=(
            jax.ShapeDtypeStruct((1, 16), F32),
            jax.ShapeDtypeStruct((8, 768), F32),
            jax.ShapeDtypeStruct((16, 768), F32),
        ),
        in_specs=[vm] * 5,
        out_specs=(vm, vm, vm),
        scratch_shapes=[
            pltpu.VMEM((3, 2, 4, 4, 4, 16, 256), BF),
            pltpu.VMEM((1024, 768), BF),
            pltpu.VMEM((1024, 768), BF),
            pltpu.VMEM((512, 768), BF),
            pltpu.VMEM((3, 2, 4, 4, 4, 16, 128), BF),
            pltpu.VMEM((3, 4, 4, 4, 16, 128), BF),
            pltpu.VMEM((3, 4, 4, 4, 16, 128), BF),
            pltpu.VMEM((3, 3, 4, 4, 16, 128), BF),
            pltpu.VMEM((3, 4, 4, 16, 128), BF),
            pltpu.VMEM((3, 3, 4, 16, 128), BF),
            pltpu.VMEM((3, 4, 16, 128), BF),
            pltpu.VMEM((3, 3, 16, 128), BF),
            pltpu.VMEM((4, 1, 1024), F32),
            pltpu.VMEM((1, 1024), F32),
            pltpu.VMEM((3, 3, 1, 1024), F32),
            dma((3, 3, 3)), dma((3, 3, 3)),
            dma((3, 7)), dma((3, 7)),
            dma((3,)), dma((3,)),
            dma((3, 3, 3)), dma((3, 3, 3)),
            dma((4, 3)), dma((4, 3)),
        ],
        compiler_params=pltpu.CompilerParams(
            collective_id=0, has_side_effects=True, vmem_limit_bytes=48 * 2**20
        ),
    )(emb, queue_states, queue_ids.reshape(1, 512), positive.reshape(1, 1024), tail_ids.reshape(1, 1024))
    return loss.reshape(16), qgrad, tgrad


def local(token_states, qkv_weight, out_weight, up_weight, down_weight, queue_states, queue_ids, positive, tail_ids):
    emb = encode(token_states[0], qkv_weight, out_weight, up_weight, down_weight).reshape(16, 768)
    return contrast(emb, queue_states, queue_ids, positive, tail_ids)


def solution(mesh):
    placed = (
        P("tower", "dp", None, None),
        P("tower", None, None, None),
        P("tower", None, None, None),
        P("tower", None, None, None),
        P("tower", None, None, None),
        P(("tower", "dp"), None),
        P(("tower", "dp")),
        P(),
        P(),
    )
    return jax.shard_map(
        local,
        mesh=mesh,
        in_specs=placed,
        out_specs=(P("dp"), P(("tower", "dp"), None), P("dp", None)),
        check_vma=False,
    )
```

```python
import functools
import jax, jax.numpy as jnp
from jax import lax
from jax.experimental import pallas as pl
from jax.experimental.pallas import tpu as pltpu
from jax.sharding import PartitionSpec as P

BF = jnp.bfloat16
F32 = jnp.float32
SEQ = 64

def dot(a, b):
    return jnp.dot(a, b, preferred_element_type=F32)

def dot_t(a, b):
    return lax.dot_general(a, b, (((1,), (1,)), ((), ())), preferred_element_type=F32)

def gelu(x):
    a = jnp.abs(x)
    t = pl.reciprocal(1.0 + (0.3275911 * 0.7071067811865476) * a, approx=True)
    p = 0.5 * 1.061405429
    for c in (-1.453152027, 1.421413741, -0.284496736, 0.254829592):
        p = p * t + 0.5 * c
    q = p * t * jnp.exp2((x * x) * (-0.5 * 1.4426950408889634))
    return jnp.maximum(x, 0.0) - a * q

def norm_rows(v):
    avg = jnp.mean(v, axis=-1, keepdims=True)
    c = v - avg
    s = jnp.mean(c * c, axis=-1, keepdims=True)
    return c * lax.rsqrt(s + 1e-5)

def unit_rows(v):
    return v * lax.rsqrt(jnp.sum(v * v, axis=-1, keepdims=True) + 1e-6)

def enc_chunk(x, wqkv, wout, wup, wdown, waits, mid, fft=768):
    m = x.shape[0]
    nt = m // SEQ
    waits[0]()
    row = lax.broadcasted_iota(jnp.int32, (256, 256), 0) // SEQ
    col = lax.broadcasted_iota(jnp.int32, (256, 256), 1) // SEQ
    ones_bd = jnp.where(row == col, 1.0, 0.0).astype(BF)
    ctx = []
    lane = lax.broadcasted_iota(jnp.int32, (SEQ, 128), 1)
    low = lane < 64
    zero = jnp.zeros((SEQ, 128), BF)
    def bd(t):
        a, b = t[:, :128], t[:, 128:]
        z = jnp.zeros_like(a)
        rows = [
            jnp.concatenate([jnp.where(low, a, z), zero], 1),
            jnp.concatenate([jnp.where(low, z, a), zero], 1),
            jnp.concatenate([zero, jnp.where(low, b, z)], 1),
            jnp.concatenate([zero, jnp.where(low, z, b)], 1),
        ]
        return jnp.concatenate(rows, 0)
    for g in range(3):
        q = (dot(x, wqkv[:, g * 256:(g + 1) * 256])).astype(BF) * BF(0.125)
        k = (dot(x, wqkv[:, 768 + g * 256:768 + (g + 1) * 256])).astype(BF)
        v = (dot(x, wqkv[:, 1536 + g * 256:1536 + (g + 1) * 256])).astype(BF)
        es = []
        for t in range(nt):
            sl = slice(t * SEQ, (t + 1) * SEQ)
            es.append(jnp.exp(dot_t(q[sl], bd(k[sl]))))
        e = jnp.concatenate(es, 0)
        p = (e / dot(e.astype(BF), ones_bd)).astype(BF)
        cs = []
        for t in range(nt):
            sl = slice(t * SEQ, (t + 1) * SEQ)
            cs.append(dot(p[sl], bd(v[sl])).astype(BF))
        ctx.append(jnp.concatenate(cs, 0))
    ctx = jnp.concatenate(ctx, 1)
    waits[1]()
    normed = norm_rows(x.astype(F32) + dot(ctx, wout[...])).astype(BF)
    waits[2]()
    acc = normed.astype(F32)
    for j in range(0, 3072, fft):
        act = gelu(dot(normed, wup[:, j:j + fft])).astype(BF)
        if j == 0:
            waits[3]()
        acc = acc + dot(act, wdown[j:j + fft, :])
        mid(j // fft)
    hid = norm_rows(acc).astype(BF).astype(F32)
    pooled = jnp.mean(hid.reshape(nt, SEQ, 768), axis=1)
    return unit_rows(pooled)

MESH = pl.DeviceIdType.MESH
INV_TEMP = 50.0


def pack(rows):
    return jnp.concatenate([rows[:, j * 128:(j + 1) * 128] for j in range(6)], axis=0)


def unpack(blocks):
    n = blocks.shape[0]
    parts = blocks.reshape(n, 6, 8, 128)
    return jnp.concatenate([parts[:, j].reshape(n * 8, 128) for j in range(6)], axis=1)


def to_row(col):
    n = col.shape[0]
    return jnp.transpose(jnp.broadcast_to(col, (n, 128)))[0:1, :]


def iota(shape, dim):
    return lax.broadcasted_iota(jnp.int32, shape, dim)


def hot(mask):
    return mask.astype(F32).astype(BF)


def step_kernel(
    x_hbm, qkv_h, out_h, up_h, down_h, queue_ref, qid_ref, pos_ref, tid_ref,
    loss_ref, qgrad_ref, tgrad_ref,
    wqkv, wout, wup, wdown, xs, keys, qids, ids, true_col, own_pack, mate_pack,
    gq, gt, queries, tails, ubuf, rbuf, qtot, tail_exp, tot_out, tot_in, grad_out, grad_in, tg_out, tg_in,
    w_sem, x_sem, agq_recv, agt_recv, ag_send, rs_send, rs_recv, tot_send, tot_recv, m_send, m_recv,
):
    tower, dp = lax.axis_index("tower"), lax.axis_index("dp")
    core, chip = lax.rem(dp, 2), lax.div(dp, 2)
    place = tower * 32 + chip
    mate = 1 - core
    mate_dev = (tower, chip * 2 + mate)
    handler = lax.rem(chip, 2) == core

    def same_core(n):
        return (lax.div(n, 32), lax.rem(n, 32) * 2 + core)

    def loop(first, last, body):
        def f(i, _):
            body(i)
            return 0
        lax.fori_loop(first, last, f, 0)

    barrier = pltpu.get_barrier_semaphore()
    loop(1, 64, lambda j: pl.semaphore_signal(barrier, inc=1, device_id=same_core(lax.rem(place + j, 64)), device_id_type=MESH))
    pl.semaphore_signal(barrier, inc=1, device_id=mate_dev, device_id_type=MESH)

    loads = [pltpu.make_async_copy(s.at[0, 0], d, w_sem.at[i]) for i, (s, d) in enumerate(
        [(qkv_h, wqkv), (out_h, wout), (up_h, wup), (down_h, wdown)])]
    x_loads = [pltpu.make_async_copy(x_hbm.at[h], xs.at[h], x_sem.at[h]) for h in range(2)]
    x_loads[0].start()
    for c in loads:
        c.start()
    x_loads[1].start()

    def remote(src, dst, ssem, rsem, dev):
        return pltpu.make_async_remote_copy(src_ref=src, dst_ref=dst, send_sem=ssem, recv_sem=rsem, device_id=dev, device_id_type=MESH)

    def key_rows(i):
        rows = pl.ds(pl.multiple_of(i * 128, 128), 128)
        keys[0, rows, :] = unit_rows(queue_ref[rows, :].astype(F32)).astype(BF)
    loop(0, 4, key_rows)
    qids[0] = qid_ref[...]
    pos = pos_ref[...]
    tid = tid_ref[...].astype(F32)
    true_row = jnp.zeros((1, 1024), F32)
    for j in range(0, 1024, 256):
        true_row = true_row + dot(jnp.broadcast_to(tid[:, j:j + 256], (16, 256)).astype(BF), hot(iota((256, 1024), 0) + j == pos))[0:1, :]
    pos_hi = lax.div(pos, 32)
    mixed = jnp.concatenate([jnp.broadcast_to(v, (8, 1024)) for v in (pos_hi.astype(F32), (pos - 32 * pos_hi).astype(F32), true_row, true_row)], axis=0).astype(BF)
    for h in range(2):
        p = iota((1024, 256), 1)
        source = (lax.div(p, 8) * 2 + core) * 16 + h * 8 + lax.rem(p, 8)
        got = dot(mixed, hot(iota((1024, 256), 0) == source))
        ids[0:1, h * 256:(h + 1) * 256] = got[0:1] * 32.0 + got[8:9]
        ids[1:2, h * 256:(h + 1) * 256] = got[16:17]
        true_col[h * 256:(h + 1) * 256, :] = jnp.transpose(jnp.broadcast_to(got[16:17], (128, 256)))

    def gather_wait(h, side, buf, sems):
        def one(s):
            @pl.when(jnp.logical_not((tower == side) & (s == chip)))
            def _():
                remote(buf.at[s], buf.at[s], ag_send.at[h, 0], sems.at[h, s], mate_dev).wait_recv()
        loop(0, 32, one)

    def gather_start(h):
        def to_all(dst, sems):
            def one(j):
                remote(own_pack.at[h], dst, ag_send.at[h, j], sems.at[h, chip], same_core(lax.rem(place + j, 64))).start()
            loop(1, 64, one)
        @pl.when(tower == 0)
        def _():
            gq[h, chip] = own_pack[h]
            to_all(gq.at[h, chip], agq_recv)
        @pl.when(tower == 1)
        def _():
            gt[h, core, chip] = own_pack[h]
            to_all(gt.at[h, core, chip], agt_recv)
        remote(own_pack.at[h], mate_pack.at[h], m_send.at[h], m_recv.at[h], mate_dev).start()

    def queue_part(h):
        gather_wait(h, 0, gq.at[h], agq_recv)
        q = unpack(gq[h].astype(F32)).astype(BF)
        queries[pl.ds(h * 256, 256), :] = q
        total = jnp.zeros((256, 1), F32)
        u = jnp.zeros((256, 768), F32)
        truth = true_col[pl.ds(h * 256, 256), 0:1]
        for who in range(2):
            k = keys[who]
            s = INV_TEMP * dot_t(q, k)
            e = jnp.where(truth != qids[who].astype(F32), jnp.exp(s), 0.0)
            total = total + jnp.sum(e, axis=1, keepdims=True)
            u = u + dot(e.astype(BF), k)
        qtot[h] = to_row(total)
        for s in range(32):
            ubuf[h, s] = pack(u[s * 8:(s + 1) * 8]).astype(BF)
        def one(s):
            dest = lax.div(s, 16) * 32 + lax.rem(2 * s + core, 32)
            @pl.when(dest == place)
            def _():
                rbuf[h, place] = ubuf[h, s]
            @pl.when(dest != place)
            def _():
                remote(ubuf.at[h, s], rbuf.at[h, place], rs_send.at[h, s], rs_recv.at[h, place], same_core(dest)).start()
        loop(0, 32, one)

    keys_copy = remote(keys.at[0], keys.at[1], m_send.at[2], m_recv.at[2], mate_dev)
    qids_copy = remote(qids.at[0], qids.at[1], m_send.at[3], m_recv.at[3], mate_dev)

    def half(h):
        def waiter(c):
            def f():
                @pl.when(h == 0)
                def _():
                    c.wait()
                    if c is loads[1]:
                        pl.semaphore_wait(barrier, 64)
            return f
        def mid(j):
            if j == MID:
                @pl.when(h == 1)
                def _():
                    keys_copy.wait_recv()
                    qids_copy.wait_recv()
                    queue_part(0)
        pltpu.make_async_copy(x_hbm.at[h], xs.at[h], x_sem.at[h]).wait()
        emb = enc_chunk(xs[h], wqkv, wout, wup, wdown, [waiter(c) for c in loads], mid)
        own_pack[h] = pack(emb).astype(BF)
        @pl.when(h == 0)
        def _():
            keys_copy.start()
            qids_copy.start()
        gather_start(h)
    loop(0, 2, half)

    def pack_wait(h):
        remote(mate_pack.at[h], mate_pack.at[h], m_send.at[h], m_recv.at[h], mate_dev).wait_recv()
    pack_wait(0)
    pack_wait(1)
    queue_part(1)

    pos_q, true_q = ids[0:1, :].astype(jnp.int32), ids[1:2, :]
    row = iota((32, 512), 0)
    is_pos = pos_q == chip * 32 + row
    chip_ids = jnp.sum(jnp.where(iota((32, 1024), 1) == chip * 32 + iota((32, 1024), 0), tid, 0.0), axis=1, keepdims=True)

    def tail_scores(mine, other):
        mine, other = unpack(mine), unpack(other)
        first = jnp.where(core == 0, mine, other)
        second = jnp.where(core == 0, other, mine)
        t32 = jnp.concatenate([first, second], axis=0).astype(BF)
        s = INV_TEMP * dot_t(t32, queries[...]) - is_pos.astype(F32)
        tail_exp[...] = jnp.where(is_pos | (chip_ids != true_q), jnp.exp(s), 0.0)

    total = jnp.concatenate([qtot[0], qtot[1]], axis=1)
    @pl.when(tower == 1)
    def _():
        tail_scores(own_pack[...].astype(F32), mate_pack[...].astype(F32))
    tail_part = jnp.sum(tail_exp[...], axis=0, keepdims=True)
    tot_out[...] = total + jnp.where(tower == 1, tail_part, 0.0)
    tot_in[place] = tot_out[...]
    loop(1, 64, lambda j: remote(tot_out, tot_in.at[place], tot_send.at[j], tot_recv.at[place], same_core(lax.rem(place + j, 64))).start())

    for h in range(2):
        gather_wait(h, 1, gt.at[h, core], agt_recv)
        remote(gt.at[h, core], gt.at[h, core], m_send.at[4 + h], m_recv.at[4 + h], mate_dev).start()
    for h in range(2):
        remote(gt.at[h, mate], gt.at[h, mate], m_send.at[4 + h], m_recv.at[4 + h], mate_dev).wait_recv()
    @pl.when(tower == 0)
    def _():
        tail_scores(gt[:, core, chip].astype(F32), gt[:, mate, chip].astype(F32))
    for who in range(2):
        halves = [unpack(gt[h, who].astype(F32)).reshape(32, 8, 768) for h in range(2)]
        tails[:, who] = jnp.concatenate(halves, axis=1).astype(BF)
    all_tails = tails[...].reshape(1024, 768)

    rows = iota((32, 1024), 0)
    lane = iota((32, 1024), 1)
    own = jnp.where(rows < 16, place * 16 + rows, dp * 16 + rows - 16)
    sel = lane == own
    own_pos = jnp.sum(jnp.where(sel, pos.astype(F32), 0.0), axis=1, keepdims=True).astype(jnp.int32)
    own_true = jnp.sum(jnp.where(sel, true_row, 0.0), axis=1, keepdims=True)
    def query_rows(d):
        return jnp.concatenate([unpack(gq[h, pl.ds(lax.div(d, 2), 1)].astype(F32)) for h in range(2)], axis=0)
    own_q = jnp.concatenate([query_rows(place), query_rows(dp)], axis=0)
    at_pos = lane == own_pos
    pos_emb = dot(hot(at_pos), all_tails)
    logit = INV_TEMP * jnp.sum(own_q * pos_emb, axis=1, keepdims=True) - 1.0
    own_s = INV_TEMP * dot_t(own_q[:16].astype(BF), all_tails)
    own_e = jnp.where(at_pos[:16] | (tid == own_true[:16]), 0.0, jnp.exp(own_s))
    from_tails = dot(own_e.astype(BF), all_tails)

    def tot_wait(s):
        @pl.when(s != place)
        def _():
            remote(tot_in.at[s], tot_in.at[s], tot_send.at[0], tot_recv.at[s], mate_dev).wait_recv()
    loop(0, 64, tot_wait)
    total = jnp.sum(tot_in[...], axis=0)

    weights = (tail_exp[...] / total - is_pos.astype(F32)).astype(BF)
    tg_out[...] = (INV_TEMP * dot(weights, queries[...])).reshape(2, 16, 768)
    tg_copy = remote(tg_out.at[mate], tg_in, m_send.at[6], m_recv.at[6], mate_dev)
    tg_copy.start()

    p = iota((32, 512), 1)
    place_of = (lax.div(lax.rem(p, 256), 8) * 2 + core) * 16 + lax.div(p, 256) * 8 + lax.rem(p, 8)
    own512 = jnp.where(iota((32, 512), 0) < 16, place * 16 + iota((32, 512), 0), dp * 16 + iota((32, 512), 0) - 16)
    own_total = jnp.sum(jnp.where(place_of == own512, total, 0.0), axis=1, keepdims=True)
    loss = jnp.log(own_total[16:]) - logit[16:]
    loss_ref[...] = jnp.sum(jnp.where(iota((16, 16), 0) == iota((16, 16), 1), loss, 0.0), axis=0, keepdims=True)

    grad_copy = remote(grad_out, grad_in, m_send.at[7], m_recv.at[7], mate_dev)
    @pl.when(handler)
    def _():
        for h in range(2):
            def rs_wait(s):
                @pl.when(s != place)
                def _():
                    remote(rbuf.at[h, s], rbuf.at[h, s], rs_send.at[h, 0], rs_recv.at[h, s], mate_dev).wait_recv()
            loop(0, 64, rs_wait)
        def add(s, acc):
            return acc + rbuf[:, s].astype(F32)
        u = unpack(lax.fori_loop(0, 64, add, jnp.zeros((2, 48, 128), F32)))
        excess = jnp.exp(logit[:16]) / own_total[:16] - 1.0
        grad = INV_TEMP * ((u + from_tails) / own_total[:16] + excess * pos_emb[:16])
        grad_out[...] = jnp.where(core == 0, grad[8:], grad[:8])
        grad_copy.start()
        qgrad_ref[...] = jnp.where(core == 0, grad[:8], grad[8:])
    @pl.when(jnp.logical_not(handler))
    def _():
        grad_copy.wait_recv()
        qgrad_ref[...] = grad_in[...]
    tg_copy.wait_recv()
    tgrad_ref[...] = jnp.where(core == 0, tg_out[0], tg_out[1]) + tg_in[...]

    @pl.when(handler)
    def _():
        grad_copy.wait_send()
    tg_copy.wait_send()
    keys_copy.wait_send()
    qids_copy.wait_send()
    for h in range(2):
        remote(own_pack.at[h], mate_pack.at[h], m_send.at[h], m_recv.at[h], mate_dev).wait_send()
        remote(gt.at[h, core], gt.at[h, core], m_send.at[4 + h], m_recv.at[4 + h], mate_dev).wait_send()
        loop(1, 64, lambda j: remote(own_pack.at[h], own_pack.at[h], ag_send.at[h, j], m_recv.at[h], mate_dev).wait_send())
        def rs_sent(s):
            @pl.when(lax.div(s, 16) * 32 + lax.rem(2 * s + core, 32) != place)
            def _():
                remote(ubuf.at[h, s], ubuf.at[h, s], rs_send.at[h, s], m_recv.at[h], mate_dev).wait_send()
        loop(0, 32, rs_sent)
    loop(1, 64, lambda j: remote(tot_out, tot_out, tot_send.at[j], m_recv.at[0], mate_dev).wait_send())


MID = 2


def local(token_states, qkv_weight, out_weight, up_weight, down_weight, queue_states, queue_ids, positive, tail_ids):
    vm, anywhere = pl.BlockSpec(memory_space=pltpu.VMEM), pl.BlockSpec(memory_space=pl.ANY)
    dma = pltpu.SemaphoreType.DMA
    loss, qgrad, tgrad = pl.pallas_call(
        step_kernel,
        out_shape=(
            jax.ShapeDtypeStruct((1, 16), F32),
            jax.ShapeDtypeStruct((8, 768), F32),
            jax.ShapeDtypeStruct((16, 768), F32),
        ),
        in_specs=[anywhere] * 5 + [vm] * 4,
        out_specs=(vm, vm, vm),
        scratch_shapes=[
            pltpu.VMEM((768, 2304), BF), pltpu.VMEM((768, 768), BF), pltpu.VMEM((768, 3072), BF), pltpu.VMEM((3072, 768), BF),
            pltpu.VMEM((2, 512, 768), BF),
            pltpu.VMEM((2, 512, 768), BF),
            pltpu.VMEM((2, 1, 512), jnp.int32),
            pltpu.VMEM((8, 512), F32),
            pltpu.VMEM((512, 128), F32),
            pltpu.VMEM((2, 48, 128), BF),
            pltpu.VMEM((2, 48, 128), BF),
            pltpu.VMEM((2, 32, 48, 128), BF),
            pltpu.VMEM((2, 2, 32, 48, 128), BF),
            pltpu.VMEM((512, 768), BF),
            pltpu.VMEM((32, 2, 16, 768), BF),
            pltpu.VMEM((2, 32, 48, 128), BF),
            pltpu.VMEM((2, 64, 48, 128), BF),
            pltpu.VMEM((2, 1, 256), F32),
            pltpu.VMEM((32, 512), F32),
            pltpu.VMEM((1, 512), F32),
            pltpu.VMEM((64, 1, 512), F32),
            pltpu.VMEM((8, 768), F32),
            pltpu.VMEM((8, 768), F32),
            pltpu.VMEM((2, 16, 768), F32),
            pltpu.VMEM((16, 768), F32),
            dma((4,)), dma((2,)), dma((2, 32)), dma((2, 32)), dma((2, 64)), dma((2, 32)), dma((2, 64)),
            dma((64,)), dma((64,)), dma((8,)), dma((8,)),
        ],
        compiler_params=pltpu.CompilerParams(
            collective_id=0, has_side_effects=True, vmem_limit_bytes=60 * 2**20
        ),
    )(token_states.reshape(2, 512, 768), qkv_weight, out_weight, up_weight, down_weight,
      queue_states, queue_ids.reshape(1, 512), positive.reshape(1, 1024), tail_ids.reshape(1, 1024))
    return loss.reshape(16), qgrad, tgrad


def solution(mesh):
    placed = (
        P("tower", "dp", None, None),
        P("tower", None, None, None),
        P("tower", None, None, None),
        P("tower", None, None, None),
        P("tower", None, None, None),
        P(("tower", "dp"), None),
        P(("tower", "dp")),
        P(),
        P(),
    )
    return jax.shard_map(
        local,
        mesh=mesh,
        in_specs=placed,
        out_specs=(P("dp"), P(("tower", "dp"), None), P("dp", None)),
        check_vma=False,
    )
```

```python
import jax
import jax.numpy as jnp
from jax import lax
from jax.experimental import pallas as pl
from jax.experimental.pallas import tpu as pltpu
from jax.sharding import PartitionSpec as P

BF = jnp.bfloat16
F32 = jnp.float32
SEQ = 64


def dot(a, b):
    return jnp.dot(a, b, preferred_element_type=F32)


def dot_t(a, b):
    return lax.dot_general(a, b, (((1,), (1,)), ((), ())), preferred_element_type=F32)


def norm_rows(v):
    avg = jnp.mean(v, axis=-1, keepdims=True)
    c = v - avg
    s = jnp.mean(c * c, axis=-1, keepdims=True)
    return c * lax.rsqrt(s + 1e-5)


def unit_rows(v):
    return v * lax.rsqrt(jnp.sum(v * v, axis=-1, keepdims=True) + 1e-6)


def gelu(x):
    return 0.5 * x * (1.0 + lax.erf(x * 0.7071067811865476))

def att_steps(out, x, wqkv, wout, waits):
    nt = x.shape[0] // SEQ
    row = lax.broadcasted_iota(jnp.int32, (256, 256), 0) // SEQ
    col = lax.broadcasted_iota(jnp.int32, (256, 256), 1) // SEQ
    ones_bd = jnp.where(row == col, 1.0, 0.0).astype(BF)
    low = lax.broadcasted_iota(jnp.int32, (SEQ, 128), 1) < 64
    zero = jnp.zeros((SEQ, 128), BF)
    def bd(t):
        a, b = t[:, :128], t[:, 128:]
        z = jnp.zeros_like(a)
        return jnp.concatenate([
            jnp.concatenate([jnp.where(low, a, z), zero], 1),
            jnp.concatenate([jnp.where(low, z, a), zero], 1),
            jnp.concatenate([zero, jnp.where(low, b, z)], 1),
            jnp.concatenate([zero, jnp.where(low, z, b)], 1)], 0)
    ctx = []
    qkv = []
    waits[0]()
    def proj(g):
        q = dot(x, wqkv[:, g * 256:(g + 1) * 256]).astype(BF) * BF(0.125)
        k = dot(x, wqkv[:, 768 + g * 256:768 + (g + 1) * 256]).astype(BF)
        v = dot(x, wqkv[:, 1536 + g * 256:1536 + (g + 1) * 256]).astype(BF)
        return q, k, v
    nxt = proj(0)
    yield
    for g in range(3):
        q, k, v = nxt
        if g < 2:
            nxt = proj(g + 1)
            yield
        es = []
        for t in range(nt):
            sl = slice(t * SEQ, (t + 1) * SEQ)
            es.append(jnp.exp(dot_t(q[sl], bd(k[sl]))))
            if t % 2: yield
        e = jnp.concatenate(es, 0)
        p = (e / dot(e.astype(BF), ones_bd)).astype(BF)
        yield
        cs = []
        for t in range(nt):
            sl = slice(t * SEQ, (t + 1) * SEQ)
            cs.append(dot(p[sl], bd(v[sl])).astype(BF))
            if t % 2: yield
        ctx.append(jnp.concatenate(cs, 0))
    ctx = jnp.concatenate(ctx, 1)
    waits[1]()
    v = x.astype(F32) + dot(ctx, wout[...])
    yield
    out["normed"] = norm_rows(v).astype(BF)

def ff_steps(out, normed, wup, wdown, waits, fft=256, nt=256):
    waits[0]()
    m = normed.shape[0]
    acts = []
    pre = dot(normed, wup[:, 0:fft])
    for j in range(0, 3072, fft):
        nxt = dot(normed, wup[:, j + fft:j + 2 * fft]) if j + fft < 3072 else None
        acts.append(gelu(pre).astype(BF))
        pre = nxt
        yield
    act = jnp.concatenate(acts, 1)
    waits[1]()
    cols = []
    for j in range(0, 768, nt):
        cols.append(normed[:, j:j + nt].astype(F32) + dot(act, wdown[:, j:j + nt]))
        yield
    hid = norm_rows(jnp.concatenate(cols, 1)).astype(BF).astype(F32)
    pooled = jnp.mean(hid.reshape(m // SEQ, SEQ, 768), axis=1)
    out["emb"] = unit_rows(pooled)

def drain(gen):
    for _ in gen: pass

def mix(a, na, b, nb):
    da = db = 0
    la = lb = True
    while la or lb:
        if la and (not lb or da * nb <= db * na):
            try: next(a); da += 1
            except StopIteration: la = False
        elif lb:
            try: next(b); db += 1
            except StopIteration: lb = False

MESH = pl.DeviceIdType.MESH
INV_TEMP = 50.0


def pack(rows):
    return jnp.concatenate([rows[:, j * 128:(j + 1) * 128] for j in range(6)], axis=0)


def unpack(blocks):
    n = blocks.shape[0]
    parts = blocks.reshape(n, 6, 8, 128)
    return jnp.concatenate([parts[:, j].reshape(n * 8, 128) for j in range(6)], axis=1)


def to_row(col):
    n = col.shape[0]
    return jnp.transpose(jnp.broadcast_to(col, (n, 128)))[0:1, :]


def iota(shape, dim):
    return lax.broadcasted_iota(jnp.int32, shape, dim)


def hot(mask):
    return mask.astype(F32).astype(BF)


def step_kernel(
    x_hbm, qkv_h, out_h, up_h, down_h, queue_ref, qid_ref, pos_ref, tid_ref,
    loss_ref, qgrad_ref, tgrad_ref,
    wqkv, wout, wup, wdown, xs, keys, qids, ids, true_col, own_pack, mate_pack,
    gq, gt, queries, tails, ubuf, rbuf, qtot, tail_exp, tot_out, tot_in, grad_out, grad_in, tg_out, tg_in,
    w_sem, x_sem, agq_recv, agt_recv, ag_send, rs_send, rs_recv, tot_send, tot_recv, m_send, m_recv,
):
    tower, dp = lax.axis_index("tower"), lax.axis_index("dp")
    core, chip = lax.rem(dp, 2), lax.div(dp, 2)
    place = tower * 32 + chip
    mate = 1 - core
    mate_dev = (tower, chip * 2 + mate)
    handler = lax.rem(chip, 2) == core

    def same_core(n):
        return (lax.div(n, 32), lax.rem(n, 32) * 2 + core)

    def loop(first, last, body):
        def f(i, _):
            body(i)
            return 0
        lax.fori_loop(first, last, f, 0)

    barrier = pltpu.get_barrier_semaphore()
    loop(1, 64, lambda j: pl.semaphore_signal(barrier, inc=1, device_id=same_core(lax.rem(place + j, 64)), device_id_type=MESH))
    pl.semaphore_signal(barrier, inc=1, device_id=mate_dev, device_id_type=MESH)

    loads = [pltpu.make_async_copy(s.at[0, 0], d, w_sem.at[i]) for i, (s, d) in enumerate(
        [(qkv_h, wqkv), (out_h, wout), (up_h, wup), (down_h, wdown)])]
    x_loads = [pltpu.make_async_copy(x_hbm.at[h], xs.at[h], x_sem.at[h]) for h in range(2)]
    x_loads[0].start()
    loads[0].start()

    def remote(src, dst, ssem, rsem, dev):
        return pltpu.make_async_remote_copy(src_ref=src, dst_ref=dst, send_sem=ssem, recv_sem=rsem, device_id=dev, device_id_type=MESH)

    def key_rows(i):
        rows = pl.ds(pl.multiple_of(i * 128, 128), 128)
        keys[0, rows, :] = unit_rows(queue_ref[rows, :].astype(F32)).astype(BF)
    loop(0, 4, key_rows)
    qids[0] = qid_ref[...]
    pos = pos_ref[...]
    tid = tid_ref[...].astype(F32)
    true_row = jnp.zeros((1, 1024), F32)
    for j in range(0, 1024, 256):
        true_row = true_row + dot(jnp.broadcast_to(tid[:, j:j + 256], (16, 256)).astype(BF), hot(iota((256, 1024), 0) + j == pos))[0:1, :]
    pos_hi = lax.div(pos, 32)
    mixed = jnp.concatenate([jnp.broadcast_to(v, (8, 1024)) for v in (pos_hi.astype(F32), (pos - 32 * pos_hi).astype(F32), true_row, true_row)], axis=0).astype(BF)
    for h in range(2):
        p = iota((1024, 256), 1)
        source = (lax.div(p, 8) * 2 + core) * 16 + h * 8 + lax.rem(p, 8)
        got = dot(mixed, hot(iota((1024, 256), 0) == source))
        ids[0:1, h * 256:(h + 1) * 256] = got[0:1] * 32.0 + got[8:9]
        ids[1:2, h * 256:(h + 1) * 256] = got[16:17]
        true_col[h * 256:(h + 1) * 256, :] = jnp.transpose(jnp.broadcast_to(got[16:17], (128, 256)))

    def arrived(ref, sem):
        remote(ref, ref, m_send.at[0], sem, mate_dev).wait_recv()

    def left(ref, sem):
        remote(ref, ref, sem, m_recv.at[0], mate_dev).wait_send()

    def gather_wait(h, side, buf, sems):
        @pl.when(tower == side)
        def _():
            arrived(buf.at[pl.ds(0, 31)], sems.at[h])
        @pl.when(tower != side)
        def _():
            arrived(buf, sems.at[h])

    def to_all(h, dst, sems):
        def one(j):
            remote(own_pack.at[h], dst, ag_send.at[h], sems.at[h], same_core(lax.rem(place + j, 64))).start()
        loop(1, 64, one)

    def send_queries(h):
        @pl.when(tower == 0)
        def _():
            gq[h, chip] = own_pack[h]
            to_all(h, gq.at[h, chip], agq_recv)
        remote(own_pack.at[h], mate_pack.at[h], m_send.at[h], m_recv.at[h], mate_dev).start()

    def send_tails(h):
        @pl.when(tower == 1)
        def _():
            gt[h, core, chip] = own_pack[h]
            to_all(h, gt.at[h, core, chip], agt_recv)

    def queue_part(h):
        gather_wait(h, 0, gq.at[h], agq_recv)
        q = unpack(gq[h].astype(F32)).astype(BF)
        queries[pl.ds(h * 256, 256), :] = q
        total = jnp.zeros((256, 1), F32)
        u = jnp.zeros((256, 768), F32)
        truth = true_col[pl.ds(h * 256, 256), 0:1]
        for who in range(2):
            k = keys[who]
            s = INV_TEMP * dot_t(q, k)
            e = jnp.where(truth != qids[who].astype(F32), jnp.exp(s), 0.0)
            total = total + jnp.sum(e, axis=1, keepdims=True)
            u = u + dot(e.astype(BF), k)
        qtot[h] = to_row(total)
        for s in range(32):
            ubuf[h, s] = pack(u[s * 8:(s + 1) * 8]).astype(BF)
        def one(s):
            dest = lax.div(s, 16) * 32 + lax.rem(2 * s + core, 32)
            @pl.when(dest == place)
            def _():
                rbuf[h, place] = ubuf[h, s]
            @pl.when(dest != place)
            def _():
                remote(ubuf.at[h, s], rbuf.at[h, place], rs_send.at[h], rs_recv.at[h], same_core(dest)).start()
        loop(0, 32, one)

    keys_copy = remote(keys.at[0], keys.at[1], m_send.at[2], m_recv.at[2], mate_dev)
    qids_copy = remote(qids.at[0], qids.at[1], m_send.at[3], m_recv.at[3], mate_dev)

    def nothing():
        pass

    def half(h):
        out = {}
        x_loads[h].wait()
        for _ in att_steps(out, xs[h], wqkv, wout, (loads[0].wait, loads[1].wait) if h == 0 else (nothing, nothing)):
            pass
        if h == 0:
            pl.semaphore_wait(barrier, 64)
            keys_copy.start()
            qids_copy.start()
        elif not EARLY:
            send_tails(0)
        for i, _ in enumerate(ff_steps(out, out["normed"], wup, wdown, (loads[2].wait, loads[3].wait) if h == 0 else (nothing, nothing))):
            if h == 1 and i == MID:
                keys_copy.wait_recv()
                qids_copy.wait_recv()
                queue_part(0)
        own_pack[h] = pack(out["emb"]).astype(BF)
        send_queries(h)
        if h == 0 and EARLY or h == 1 and not LATE:
            send_tails(h)

    for c in loads[1:]:
        c.start()
    x_loads[1].start()
    half(0)
    half(1)
    if MID is None:
        keys_copy.wait_recv()
        qids_copy.wait_recv()
        queue_part(0)

    def pack_wait(h):
        remote(mate_pack.at[h], mate_pack.at[h], m_send.at[h], m_recv.at[h], mate_dev).wait_recv()
    pack_wait(0)
    pack_wait(1)
    queue_part(1)
    if LATE == 1:
        send_tails(1)

    pos_q, true_q = ids[0:1, :].astype(jnp.int32), ids[1:2, :]
    row = iota((32, 512), 0)
    is_pos = pos_q == chip * 32 + row
    chip_ids = jnp.sum(jnp.where(iota((32, 1024), 1) == chip * 32 + iota((32, 1024), 0), tid, 0.0), axis=1, keepdims=True)

    def tail_scores(mine, other):
        mine, other = unpack(mine), unpack(other)
        first = jnp.where(core == 0, mine, other)
        second = jnp.where(core == 0, other, mine)
        t32 = jnp.concatenate([first, second], axis=0).astype(BF)
        s = INV_TEMP * dot_t(t32, queries[...]) - is_pos.astype(F32)
        tail_exp[...] = jnp.where(is_pos | (chip_ids != true_q), jnp.exp(s), 0.0)

    total = jnp.concatenate([qtot[0], qtot[1]], axis=1)
    @pl.when(tower == 1)
    def _():
        tail_scores(own_pack[...].astype(F32), mate_pack[...].astype(F32))
    tail_part = jnp.sum(tail_exp[...], axis=0, keepdims=True)
    tot_out[...] = total + jnp.where(tower == 1, tail_part, 0.0)
    tot_in[place] = tot_out[...]
    loop(1, 64, lambda j: remote(tot_out, tot_in.at[place], tot_send.at[0], tot_recv.at[0], same_core(lax.rem(place + j, 64))).start())

    if LATE == 2:
        send_tails(1)

    for h in range(2):
        gather_wait(h, 1, gt.at[h, core], agt_recv)
        remote(gt.at[h, core], gt.at[h, core], m_send.at[4 + h], m_recv.at[4 + h], mate_dev).start()
    for h in range(2):
        remote(gt.at[h, mate], gt.at[h, mate], m_send.at[4 + h], m_recv.at[4 + h], mate_dev).wait_recv()
    @pl.when(tower == 0)
    def _():
        tail_scores(gt[:, core, chip].astype(F32), gt[:, mate, chip].astype(F32))
    for who in range(2):
        halves = [unpack(gt[h, who].astype(F32)).reshape(32, 8, 768) for h in range(2)]
        tails[:, who] = jnp.concatenate(halves, axis=1).astype(BF)
    all_tails = tails[...].reshape(1024, 768)

    rows = iota((32, 1024), 0)
    lane = iota((32, 1024), 1)
    own = jnp.where(rows < 16, place * 16 + rows, dp * 16 + rows - 16)
    sel = lane == own
    own_pos = jnp.sum(jnp.where(sel, pos.astype(F32), 0.0), axis=1, keepdims=True).astype(jnp.int32)
    own_true = jnp.sum(jnp.where(sel, true_row, 0.0), axis=1, keepdims=True)
    def query_rows(d):
        return jnp.concatenate([unpack(gq[h, pl.ds(lax.div(d, 2), 1)].astype(F32)) for h in range(2)], axis=0)
    own_q = jnp.concatenate([query_rows(place), query_rows(dp)], axis=0)
    at_pos = lane == own_pos
    pos_emb = dot(hot(at_pos), all_tails)
    logit = INV_TEMP * jnp.sum(own_q * pos_emb, axis=1, keepdims=True) - 1.0
    own_s = INV_TEMP * dot_t(own_q[:16].astype(BF), all_tails)
    own_e = jnp.where(at_pos[:16] | (tid == own_true[:16]), 0.0, jnp.exp(own_s))
    from_tails = dot(own_e.astype(BF), all_tails)

    for h in range(2):
        left(rbuf.at[h, pl.ds(0, 63)], ag_send.at[h])
        @pl.when(handler)
        def _():
            left(ubuf.at[h, pl.ds(0, 31)], rs_send.at[h])
        @pl.when(jnp.logical_not(handler))
        def _():
            left(ubuf.at[h], rs_send.at[h])
        left(mate_pack.at[h], m_send.at[h])
        left(gt.at[h, core], m_send.at[4 + h])
    keys_copy.wait_send()
    qids_copy.wait_send()
    left(tot_in.at[pl.ds(0, 63)], tot_send.at[0])

    arrived(tot_in.at[pl.ds(0, 63)], tot_recv.at[0])
    total = jnp.sum(tot_in[...], axis=0)

    weights = (tail_exp[...] / total - is_pos.astype(F32)).astype(BF)
    tg_out[...] = (INV_TEMP * dot(weights, queries[...])).reshape(2, 16, 768)
    tg_copy = remote(tg_out.at[mate], tg_in, m_send.at[6], m_recv.at[6], mate_dev)
    tg_copy.start()

    p = iota((32, 512), 1)
    place_of = (lax.div(lax.rem(p, 256), 8) * 2 + core) * 16 + lax.div(p, 256) * 8 + lax.rem(p, 8)
    own512 = jnp.where(iota((32, 512), 0) < 16, place * 16 + iota((32, 512), 0), dp * 16 + iota((32, 512), 0) - 16)
    own_total = jnp.sum(jnp.where(place_of == own512, total, 0.0), axis=1, keepdims=True)
    loss = jnp.log(own_total[16:]) - logit[16:]
    loss_ref[...] = jnp.sum(jnp.where(iota((16, 16), 0) == iota((16, 16), 1), loss, 0.0), axis=0, keepdims=True)

    grad_copy = remote(grad_out, grad_in, m_send.at[7], m_recv.at[7], mate_dev)
    @pl.when(handler)
    def _():
        for h in range(2):
            arrived(rbuf.at[h, pl.ds(0, 63)], rs_recv.at[h])
        def add(s, acc):
            return acc + rbuf[:, s].astype(F32)
        u = unpack(lax.fori_loop(0, 64, add, jnp.zeros((2, 48, 128), F32)))
        excess = jnp.exp(logit[:16]) / own_total[:16] - 1.0
        grad = INV_TEMP * ((u + from_tails) / own_total[:16] + excess * pos_emb[:16])
        grad_out[...] = jnp.where(core == 0, grad[8:], grad[:8])
        grad_copy.start()
        qgrad_ref[...] = jnp.where(core == 0, grad[:8], grad[8:])
    @pl.when(jnp.logical_not(handler))
    def _():
        grad_copy.wait_recv()
        qgrad_ref[...] = grad_in[...]
    tg_copy.wait_recv()
    tgrad_ref[...] = jnp.where(core == 0, tg_out[0], tg_out[1]) + tg_in[...]

    @pl.when(handler)
    def _():
        grad_copy.wait_send()
    tg_copy.wait_send()


MID = 11
LATE = 0
VM = 60
EARLY = False


def local(token_states, qkv_weight, out_weight, up_weight, down_weight, queue_states, queue_ids, positive, tail_ids):
    vm, anywhere = pl.BlockSpec(memory_space=pltpu.VMEM), pl.BlockSpec(memory_space=pl.ANY)
    dma = pltpu.SemaphoreType.DMA
    loss, qgrad, tgrad = pl.pallas_call(
        step_kernel,
        out_shape=(
            jax.ShapeDtypeStruct((1, 16), F32),
            jax.ShapeDtypeStruct((8, 768), F32),
            jax.ShapeDtypeStruct((16, 768), F32),
        ),
        in_specs=[anywhere] * 5 + [vm] * 4,
        out_specs=(vm, vm, vm),
        scratch_shapes=[
            pltpu.VMEM((768, 2304), BF), pltpu.VMEM((768, 768), BF), pltpu.VMEM((768, 3072), BF), pltpu.VMEM((3072, 768), BF),
            pltpu.VMEM((2, 512, 768), BF),
            pltpu.VMEM((2, 512, 768), BF),
            pltpu.VMEM((2, 1, 512), jnp.int32),
            pltpu.VMEM((8, 512), F32),
            pltpu.VMEM((512, 128), F32),
            pltpu.VMEM((2, 48, 128), BF),
            pltpu.VMEM((2, 48, 128), BF),
            pltpu.VMEM((2, 32, 48, 128), BF),
            pltpu.VMEM((2, 2, 32, 48, 128), BF),
            pltpu.VMEM((512, 768), BF),
            pltpu.VMEM((32, 2, 16, 768), BF),
            pltpu.VMEM((2, 32, 48, 128), BF),
            pltpu.VMEM((2, 64, 48, 128), BF),
            pltpu.VMEM((2, 1, 256), F32),
            pltpu.VMEM((32, 512), F32),
            pltpu.VMEM((1, 512), F32),
            pltpu.VMEM((64, 1, 512), F32),
            pltpu.VMEM((8, 768), F32),
            pltpu.VMEM((8, 768), F32),
            pltpu.VMEM((2, 16, 768), F32),
            pltpu.VMEM((16, 768), F32),
            dma((4,)), dma((2,)), dma((2,)), dma((2,)), dma((2,)), dma((2,)), dma((2,)),
            dma((1,)), dma((1,)), dma((8,)), dma((8,)),
        ],
        compiler_params=pltpu.CompilerParams(
            collective_id=0, has_side_effects=True, vmem_limit_bytes=VM * 2**20
        ),
    )(token_states.reshape(2, 512, 768), qkv_weight, out_weight, up_weight, down_weight,
      queue_states, queue_ids.reshape(1, 512), positive.reshape(1, 1024), tail_ids.reshape(1, 1024))
    return loss.reshape(16), qgrad, tgrad


def solution(mesh):
    placed = (
        P("tower", "dp", None, None),
        P("tower", None, None, None),
        P("tower", None, None, None),
        P("tower", None, None, None),
        P("tower", None, None, None),
        P(("tower", "dp"), None),
        P(("tower", "dp")),
        P(),
        P(),
    )
    return jax.shard_map(
        local,
        mesh=mesh,
        in_specs=placed,
        out_specs=(P("dp"), P(("tower", "dp"), None), P("dp", None)),
        check_vma=False,
    )
```

```python
import jax
import jax.numpy as jnp
from jax import lax
from jax.experimental import pallas as pl
from jax.experimental.pallas import tpu as pltpu
from jax.sharding import PartitionSpec as P

BF = jnp.bfloat16
F32 = jnp.float32
SEQ = 64


def dot(a, b):
    return jnp.dot(a, b, preferred_element_type=F32)


def dot_t(a, b):
    return lax.dot_general(a, b, (((1,), (1,)), ((), ())), preferred_element_type=F32)


def norm_rows(v):
    avg = jnp.mean(v, axis=-1, keepdims=True)
    c = v - avg
    s = jnp.mean(c * c, axis=-1, keepdims=True)
    return c * lax.rsqrt(s + 1e-5)


def unit_rows(v):
    return v * lax.rsqrt(jnp.sum(v * v, axis=-1, keepdims=True) + 1e-6)


def gelu(x):
    return 0.5 * x * (1.0 + lax.erf(x * 0.7071067811865476))

def att_steps(out, x, wqkv, wout, waits):
    nt = x.shape[0] // SEQ
    row = lax.broadcasted_iota(jnp.int32, (256, 256), 0) // SEQ
    col = lax.broadcasted_iota(jnp.int32, (256, 256), 1) // SEQ
    ones_bd = jnp.where(row == col, 1.0, 0.0).astype(BF)
    low = lax.broadcasted_iota(jnp.int32, (SEQ, 128), 1) < 64
    zero = jnp.zeros((SEQ, 128), BF)
    def bd(t):
        a, b = t[:, :128], t[:, 128:]
        z = jnp.zeros_like(a)
        return jnp.concatenate([
            jnp.concatenate([jnp.where(low, a, z), zero], 1),
            jnp.concatenate([jnp.where(low, z, a), zero], 1),
            jnp.concatenate([zero, jnp.where(low, b, z)], 1),
            jnp.concatenate([zero, jnp.where(low, z, b)], 1)], 0)
    ctx = []
    qkv = []
    waits[0]()
    def proj(g):
        q = dot(x, wqkv[:, g * 256:(g + 1) * 256]).astype(BF) * BF(0.125)
        k = dot(x, wqkv[:, 768 + g * 256:768 + (g + 1) * 256]).astype(BF)
        v = dot(x, wqkv[:, 1536 + g * 256:1536 + (g + 1) * 256]).astype(BF)
        return q, k, v
    nxt = proj(0)
    yield
    for g in range(3):
        q, k, v = nxt
        if g < 2:
            nxt = proj(g + 1)
            yield
        es = []
        for t in range(nt):
            sl = slice(t * SEQ, (t + 1) * SEQ)
            es.append(jnp.exp(dot_t(q[sl], bd(k[sl]))))
            if t % 2: yield
        e = jnp.concatenate(es, 0)
        p = (e / dot(e.astype(BF), ones_bd)).astype(BF)
        yield
        cs = []
        for t in range(nt):
            sl = slice(t * SEQ, (t + 1) * SEQ)
            cs.append(dot(p[sl], bd(v[sl])).astype(BF))
            if t % 2: yield
        ctx.append(jnp.concatenate(cs, 0))
    ctx = jnp.concatenate(ctx, 1)
    waits[1]()
    v = x.astype(F32) + dot(ctx, wout[...])
    yield
    out["normed"] = norm_rows(v).astype(BF)

def ff_steps(out, normed, wup, wdown, waits, fft=256, nt=256):
    waits[0]()
    m = normed.shape[0]
    acts = []
    pre = dot(normed, wup[:, 0:fft])
    for j in range(0, 3072, fft):
        nxt = dot(normed, wup[:, j + fft:j + 2 * fft]) if j + fft < 3072 else None
        acts.append(gelu(pre).astype(BF))
        pre = nxt
        yield
    act = jnp.concatenate(acts, 1)
    waits[1]()
    cols = []
    for j in range(0, 768, nt):
        cols.append(normed[:, j:j + nt].astype(F32) + dot(act, wdown[:, j:j + nt]))
        yield
    hid = norm_rows(jnp.concatenate(cols, 1)).astype(BF).astype(F32)
    pooled = jnp.mean(hid.reshape(m // SEQ, SEQ, 768), axis=1)
    out["emb"] = unit_rows(pooled)

def drain(gen):
    for _ in gen: pass

def mix(a, na, b, nb):
    da = db = 0
    la = lb = True
    while la or lb:
        if la and (not lb or da * nb <= db * na):
            try: next(a); da += 1
            except StopIteration: la = False
        elif lb:
            try: next(b); db += 1
            except StopIteration: lb = False

MESH = pl.DeviceIdType.MESH
INV_TEMP = 50.0


def pack(rows):
    return jnp.concatenate([rows[:, j * 128:(j + 1) * 128] for j in range(6)], axis=0)


def unpack(blocks):
    n = blocks.shape[0]
    parts = blocks.reshape(n, 6, 8, 128)
    return jnp.concatenate([parts[:, j].reshape(n * 8, 128) for j in range(6)], axis=1)


def to_row(col):
    n = col.shape[0]
    return jnp.transpose(jnp.broadcast_to(col, (n, 128)))[0:1, :]


def iota(shape, dim):
    return lax.broadcasted_iota(jnp.int32, shape, dim)


def hot(mask):
    return mask.astype(F32).astype(BF)


def step_kernel(
    x_hbm, qkv_h, out_h, up_h, down_h, queue_ref, qid_ref, pos_ref, tid_ref,
    loss_ref, qgrad_ref, tgrad_ref,
    wqkv, wout, wup, wdown, xs, keys, qids, ids, true_col, own_pack, mate_pack,
    gq, gt, queries, tails, ubuf, rbuf, qtot, tail_exp, tot_out, tot_in, grad_out, grad_in, tg_out, tg_in,
    w_sem, x_sem, agq_recv, agt_recv, ag_send, rs_send, rs_recv, tot_send, tot_recv, m_send, m_recv,
):
    tower, dp = lax.axis_index("tower"), lax.axis_index("dp")
    core, chip = lax.rem(dp, 2), lax.div(dp, 2)
    place = tower * 32 + chip
    mate = 1 - core
    mate_dev = (tower, chip * 2 + mate)
    handler = lax.rem(chip, 2) == core

    def same_core(n):
        return (lax.div(n, 32), lax.rem(n, 32) * 2 + core)

    def loop(first, last, body):
        def f(i, _):
            body(i)
            return 0
        lax.fori_loop(first, last, f, 0)

    barrier = pltpu.get_barrier_semaphore()
    loop(1, 64, lambda j: pl.semaphore_signal(barrier, inc=1, device_id=same_core(lax.rem(place + j, 64)), device_id_type=MESH))
    pl.semaphore_signal(barrier, inc=1, device_id=mate_dev, device_id_type=MESH)

    loads = [pltpu.make_async_copy(s.at[0, 0], d, w_sem.at[i]) for i, (s, d) in enumerate(
        [(qkv_h, wqkv), (out_h, wout), (up_h, wup), (down_h, wdown)])]
    x_loads = [pltpu.make_async_copy(x_hbm.at[h], xs.at[h], x_sem.at[h]) for h in range(2)]
    x_loads[0].start()
    loads[0].start()

    def remote(src, dst, ssem, rsem, dev):
        return pltpu.make_async_remote_copy(src_ref=src, dst_ref=dst, send_sem=ssem, recv_sem=rsem, device_id=dev, device_id_type=MESH)

    def key_rows(i):
        rows = pl.ds(pl.multiple_of(i * 128, 128), 128)
        keys[0, rows, :] = unit_rows(queue_ref[rows, :].astype(F32)).astype(BF)
    loop(0, 4, key_rows)
    qids[0] = qid_ref[...]
    pos = pos_ref[...]
    tid = tid_ref[...].astype(F32)
    true_row = jnp.zeros((1, 1024), F32)
    for j in range(0, 1024, 256):
        true_row = true_row + dot(jnp.broadcast_to(tid[:, j:j + 256], (16, 256)).astype(BF), hot(iota((256, 1024), 0) + j == pos))[0:1, :]
    pos_hi = lax.div(pos, 32)
    mixed = jnp.concatenate([jnp.broadcast_to(v, (8, 1024)) for v in (pos_hi.astype(F32), (pos - 32 * pos_hi).astype(F32), true_row, true_row)], axis=0).astype(BF)
    for h in range(2):
        p = iota((1024, 256), 1)
        source = (lax.div(p, 8) * 2 + core) * 16 + h * 8 + lax.rem(p, 8)
        got = dot(mixed, hot(iota((1024, 256), 0) == source))
        ids[0:1, h * 256:(h + 1) * 256] = got[0:1] * 32.0 + got[8:9]
        ids[1:2, h * 256:(h + 1) * 256] = got[16:17]
        true_col[h * 256:(h + 1) * 256, :] = jnp.transpose(jnp.broadcast_to(got[16:17], (128, 256)))

    def arrived(ref, sem):
        remote(ref, ref, m_send.at[0], sem, mate_dev).wait_recv()

    def left(ref, sem):
        remote(ref, ref, sem, m_recv.at[0], mate_dev).wait_send()

    def gather_wait(h, side, buf, sems):
        @pl.when(tower == side)
        def _():
            arrived(buf.at[pl.ds(0, 31)], sems.at[h])
        @pl.when(tower != side)
        def _():
            arrived(buf, sems.at[h])

    def to_all(h, dst, sems):
        def one(j):
            remote(own_pack.at[h], dst, ag_send.at[h], sems.at[h], same_core(lax.rem(place + HOP * j, 64))).start()
        loop(1, 64, one)

    def send_queries(h):
        @pl.when(tower == 0)
        def _():
            gq[h, chip] = own_pack[h]
            to_all(h, gq.at[h, chip], agq_recv)
        remote(own_pack.at[h], mate_pack.at[h], m_send.at[h], m_recv.at[h], mate_dev).start()

    def send_tails(h):
        @pl.when(tower == 1)
        def _():
            gt[h, core, chip] = own_pack[h]
            to_all(h, gt.at[h, core, chip], agt_recv)

    def queue_part(h):
        gather_wait(h, 0, gq.at[h], agq_recv)
        q = unpack(gq[h].astype(F32)).astype(BF)
        queries[pl.ds(h * 256, 256), :] = q
        total = jnp.zeros((256, 1), F32)
        u = jnp.zeros((256, 768), F32)
        truth = true_col[pl.ds(h * 256, 256), 0:1]
        for who in range(2):
            k = keys[who]
            s = INV_TEMP * dot_t(q, k)
            e = jnp.where(truth != qids[who].astype(F32), jnp.exp(s), 0.0)
            total = total + jnp.sum(e, axis=1, keepdims=True)
            u = u + dot(e.astype(BF), k)
        qtot[h] = to_row(total)
        for s in range(32):
            ubuf[h, s] = pack(u[s * 8:(s + 1) * 8]).astype(BF)
        def one(j):
            s = lax.rem(j * STRIDE + chip, 32)
            dest = lax.div(s, 16) * 32 + lax.rem(2 * s + core, 32)
            @pl.when(dest == place)
            def _():
                rbuf[h, place] = ubuf[h, s]
            @pl.when(dest != place)
            def _():
                remote(ubuf.at[h, s], rbuf.at[h, place], rs_send.at[h], rs_recv.at[h], same_core(dest)).start()
        loop(0, 32, one)

    keys_copy = remote(keys.at[0], keys.at[1], m_send.at[2], m_recv.at[2], mate_dev)
    qids_copy = remote(qids.at[0], qids.at[1], m_send.at[3], m_recv.at[3], mate_dev)

    def nothing():
        pass

    def half(h):
        out = {}
        x_loads[h].wait()
        for _ in att_steps(out, xs[h], wqkv, wout, (loads[0].wait, loads[1].wait) if h == 0 else (nothing, nothing)):
            pass
        if h == 0:
            pl.semaphore_wait(barrier, 64)
            keys_copy.start()
            qids_copy.start()
        elif not EARLY:
            send_tails(0)
        for i, _ in enumerate(ff_steps(out, out["normed"], wup, wdown, (loads[2].wait, loads[3].wait) if h == 0 else (nothing, nothing))):
            if h == 1 and i == MID:
                keys_copy.wait_recv()
                qids_copy.wait_recv()
                queue_part(0)
        own_pack[h] = pack(out["emb"]).astype(BF)
        send_queries(h)
        if h == 0 and EARLY or h == 1 and not LATE:
            send_tails(h)

    for c in loads[1:]:
        c.start()
    x_loads[1].start()
    half(0)
    half(1)
    if MID is None:
        keys_copy.wait_recv()
        qids_copy.wait_recv()
        queue_part(0)

    def pack_wait(h):
        remote(mate_pack.at[h], mate_pack.at[h], m_send.at[h], m_recv.at[h], mate_dev).wait_recv()
    pack_wait(0)
    pack_wait(1)
    queue_part(1)
    if LATE == 1:
        send_tails(1)

    pos_q, true_q = ids[0:1, :].astype(jnp.int32), ids[1:2, :]
    row = iota((32, 512), 0)
    is_pos = pos_q == chip * 32 + row
    chip_ids = jnp.sum(jnp.where(iota((32, 1024), 1) == chip * 32 + iota((32, 1024), 0), tid, 0.0), axis=1, keepdims=True)

    def tail_scores(mine, other):
        mine, other = unpack(mine), unpack(other)
        first = jnp.where(core == 0, mine, other)
        second = jnp.where(core == 0, other, mine)
        t32 = jnp.concatenate([first, second], axis=0).astype(BF)
        s = INV_TEMP * dot_t(t32, queries[...]) - is_pos.astype(F32)
        tail_exp[...] = jnp.where(is_pos | (chip_ids != true_q), jnp.exp(s), 0.0)

    total = jnp.concatenate([qtot[0], qtot[1]], axis=1)
    @pl.when(tower == 1)
    def _():
        tail_scores(own_pack[...].astype(F32), mate_pack[...].astype(F32))
    tail_part = jnp.sum(tail_exp[...], axis=0, keepdims=True)
    tot_out[...] = total + jnp.where(tower == 1, tail_part, 0.0)
    tot_in[place] = tot_out[...]
    loop(1, 64, lambda j: remote(tot_out, tot_in.at[place], tot_send.at[0], tot_recv.at[0], same_core(lax.rem(place + HOP * j, 64))).start())

    if LATE == 2:
        send_tails(1)

    for h in range(2):
        gather_wait(h, 1, gt.at[h, core], agt_recv)
        remote(gt.at[h, core], gt.at[h, core], m_send.at[4 + h], m_recv.at[4 + h], mate_dev).start()
    for h in range(2):
        remote(gt.at[h, mate], gt.at[h, mate], m_send.at[4 + h], m_recv.at[4 + h], mate_dev).wait_recv()
    @pl.when(tower == 0)
    def _():
        tail_scores(gt[:, core, chip].astype(F32), gt[:, mate, chip].astype(F32))
    for who in range(2):
        halves = [unpack(gt[h, who].astype(F32)).reshape(32, 8, 768) for h in range(2)]
        tails[:, who] = jnp.concatenate(halves, axis=1).astype(BF)
    all_tails = tails[...].reshape(1024, 768)

    rows = iota((32, 1024), 0)
    lane = iota((32, 1024), 1)
    own = jnp.where(rows < 16, place * 16 + rows, dp * 16 + rows - 16)
    sel = lane == own
    own_pos = jnp.sum(jnp.where(sel, pos.astype(F32), 0.0), axis=1, keepdims=True).astype(jnp.int32)
    own_true = jnp.sum(jnp.where(sel, true_row, 0.0), axis=1, keepdims=True)
    def query_rows(d):
        return jnp.concatenate([unpack(gq[h, pl.ds(lax.div(d, 2), 1)].astype(F32)) for h in range(2)], axis=0)
    own_q = jnp.concatenate([query_rows(place), query_rows(dp)], axis=0)
    at_pos = lane == own_pos
    pos_emb = dot(hot(at_pos), all_tails)
    logit = INV_TEMP * jnp.sum(own_q * pos_emb, axis=1, keepdims=True) - 1.0
    own_s = INV_TEMP * dot_t(own_q[:16].astype(BF), all_tails)
    own_e = jnp.where(at_pos[:16] | (tid == own_true[:16]), 0.0, jnp.exp(own_s))
    from_tails = dot(own_e.astype(BF), all_tails)

    for h in range(2):
        left(rbuf.at[h, pl.ds(0, 63)], ag_send.at[h])
        @pl.when(handler)
        def _():
            left(ubuf.at[h, pl.ds(0, 31)], rs_send.at[h])
        @pl.when(jnp.logical_not(handler))
        def _():
            left(ubuf.at[h], rs_send.at[h])
        left(mate_pack.at[h], m_send.at[h])
        left(gt.at[h, core], m_send.at[4 + h])
    keys_copy.wait_send()
    qids_copy.wait_send()
    left(tot_in.at[pl.ds(0, 63)], tot_send.at[0])

    arrived(tot_in.at[pl.ds(0, 63)], tot_recv.at[0])
    total = jnp.sum(tot_in[...], axis=0)

    weights = (tail_exp[...] / total - is_pos.astype(F32)).astype(BF)
    tg_out[...] = (INV_TEMP * dot(weights, queries[...])).reshape(2, 16, 768)
    tg_copy = remote(tg_out.at[mate], tg_in, m_send.at[6], m_recv.at[6], mate_dev)
    tg_copy.start()

    p = iota((32, 512), 1)
    place_of = (lax.div(lax.rem(p, 256), 8) * 2 + core) * 16 + lax.div(p, 256) * 8 + lax.rem(p, 8)
    own512 = jnp.where(iota((32, 512), 0) < 16, place * 16 + iota((32, 512), 0), dp * 16 + iota((32, 512), 0) - 16)
    own_total = jnp.sum(jnp.where(place_of == own512, total, 0.0), axis=1, keepdims=True)
    loss = jnp.log(own_total[16:]) - logit[16:]
    loss_ref[...] = jnp.sum(jnp.where(iota((16, 16), 0) == iota((16, 16), 1), loss, 0.0), axis=0, keepdims=True)

    grad_copy = remote(grad_out, grad_in, m_send.at[7], m_recv.at[7], mate_dev)
    @pl.when(handler)
    def _():
        def summed(h):
            arrived(rbuf.at[h, pl.ds(0, 63)], rs_recv.at[h])
            def add(s, acc):
                for i in range(4):
                    acc = acc + rbuf[h, s * 4 + i].astype(F32)
                return acc
            return lax.fori_loop(0, 16, add, jnp.zeros((48, 128), F32))
        u = unpack(jnp.stack([summed(0), summed(1)]))
        excess = jnp.exp(logit[:16]) / own_total[:16] - 1.0
        grad = INV_TEMP * ((u + from_tails) / own_total[:16] + excess * pos_emb[:16])
        grad_out[...] = jnp.where(core == 0, grad[8:], grad[:8])
        grad_copy.start()
        qgrad_ref[...] = jnp.where(core == 0, grad[:8], grad[8:])
    @pl.when(jnp.logical_not(handler))
    def _():
        grad_copy.wait_recv()
        qgrad_ref[...] = grad_in[...]
    tg_copy.wait_recv()
    tgrad_ref[...] = jnp.where(core == 0, tg_out[0], tg_out[1]) + tg_in[...]

    @pl.when(handler)
    def _():
        grad_copy.wait_send()
    tg_copy.wait_send()


MID = 11
STRIDE = 5
HOP = 21
LATE = 0
VM = 60
EARLY = False


def local(token_states, qkv_weight, out_weight, up_weight, down_weight, queue_states, queue_ids, positive, tail_ids):
    vm, anywhere = pl.BlockSpec(memory_space=pltpu.VMEM), pl.BlockSpec(memory_space=pl.ANY)
    dma = pltpu.SemaphoreType.DMA
    loss, qgrad, tgrad = pl.pallas_call(
        step_kernel,
        out_shape=(
            jax.ShapeDtypeStruct((1, 16), F32),
            jax.ShapeDtypeStruct((8, 768), F32),
            jax.ShapeDtypeStruct((16, 768), F32),
        ),
        in_specs=[anywhere] * 5 + [vm] * 4,
        out_specs=(vm, vm, vm),
        scratch_shapes=[
            pltpu.VMEM((768, 2304), BF), pltpu.VMEM((768, 768), BF), pltpu.VMEM((768, 3072), BF), pltpu.VMEM((3072, 768), BF),
            pltpu.VMEM((2, 512, 768), BF),
            pltpu.VMEM((2, 512, 768), BF),
            pltpu.VMEM((2, 1, 512), jnp.int32),
            pltpu.VMEM((8, 512), F32),
            pltpu.VMEM((512, 128), F32),
            pltpu.VMEM((2, 48, 128), BF),
            pltpu.VMEM((2, 48, 128), BF),
            pltpu.VMEM((2, 32, 48, 128), BF),
            pltpu.VMEM((2, 2, 32, 48, 128), BF),
            pltpu.VMEM((512, 768), BF),
            pltpu.VMEM((32, 2, 16, 768), BF),
            pltpu.VMEM((2, 32, 48, 128), BF),
            pltpu.VMEM((2, 64, 48, 128), BF),
            pltpu.VMEM((2, 1, 256), F32),
            pltpu.VMEM((32, 512), F32),
            pltpu.VMEM((1, 512), F32),
            pltpu.VMEM((64, 1, 512), F32),
            pltpu.VMEM((8, 768), F32),
            pltpu.VMEM((8, 768), F32),
            pltpu.VMEM((2, 16, 768), F32),
            pltpu.VMEM((16, 768), F32),
            dma((4,)), dma((2,)), dma((2,)), dma((2,)), dma((2,)), dma((2,)), dma((2,)),
            dma((1,)), dma((1,)), dma((8,)), dma((8,)),
        ],
        compiler_params=pltpu.CompilerParams(
            collective_id=0, has_side_effects=True, vmem_limit_bytes=VM * 2**20
        ),
    )(token_states.reshape(2, 512, 768), qkv_weight, out_weight, up_weight, down_weight,
      queue_states, queue_ids.reshape(1, 512), positive.reshape(1, 1024), tail_ids.reshape(1, 1024))
    def finish(*refs):
        for src, dst in zip(refs[:3], refs[3:]):
            dst[...] = src[...]
    loss, qgrad, tgrad = pl.pallas_call(
        finish,
        out_shape=tuple(jax.ShapeDtypeStruct(v.shape, F32) for v in (loss, qgrad, tgrad)),
        in_specs=[vm] * 3,
        out_specs=(vm, vm, vm),
    )(loss, qgrad, tgrad)
    return loss.reshape(16), qgrad, tgrad


def solution(mesh):
    placed = (
        P("tower", "dp", None, None),
        P("tower", None, None, None),
        P("tower", None, None, None),
        P("tower", None, None, None),
        P("tower", None, None, None),
        P(("tower", "dp"), None),
        P(("tower", "dp")),
        P(),
        P(),
    )
    return jax.shard_map(
        local,
        mesh=mesh,
        in_specs=placed,
        out_specs=(P("dp"), P(("tower", "dp"), None), P("dp", None)),
        check_vma=False,
    )
```

```python
import jax
import jax.numpy as jnp
from jax import lax
from jax.experimental import pallas as pl
from jax.experimental.pallas import tpu as pltpu
from jax.sharding import PartitionSpec as P

BF = jnp.bfloat16
F32 = jnp.float32
SEQ = 64


def dot(a, b):
    return jnp.dot(a, b, preferred_element_type=F32)


def dot_t(a, b):
    return lax.dot_general(a, b, (((1,), (1,)), ((), ())), preferred_element_type=F32)


def norm_rows(v):
    avg = jnp.mean(v, axis=-1, keepdims=True)
    c = v - avg
    s = jnp.mean(c * c, axis=-1, keepdims=True)
    return c * lax.rsqrt(s + 1e-5)


def unit_rows(v):
    return v * lax.rsqrt(jnp.sum(v * v, axis=-1, keepdims=True) + 1e-6)


def gelu(x):
    return 0.5 * x * (1.0 + lax.erf(x * 0.7071067811865476))

def att_steps(out, x, wqkv, wout, waits):
    nt = x.shape[0] // SEQ
    row = lax.broadcasted_iota(jnp.int32, (256, 256), 0) // SEQ
    col = lax.broadcasted_iota(jnp.int32, (256, 256), 1) // SEQ
    ones_bd = jnp.where(row == col, 1.0, 0.0).astype(BF)
    low = lax.broadcasted_iota(jnp.int32, (SEQ, 128), 1) < 64
    zero = jnp.zeros((SEQ, 128), BF)
    def bd(t):
        a, b = t[:, :128], t[:, 128:]
        z = jnp.zeros_like(a)
        return jnp.concatenate([
            jnp.concatenate([jnp.where(low, a, z), zero], 1),
            jnp.concatenate([jnp.where(low, z, a), zero], 1),
            jnp.concatenate([zero, jnp.where(low, b, z)], 1),
            jnp.concatenate([zero, jnp.where(low, z, b)], 1)], 0)
    ctx = []
    qkv = []
    waits[0]()
    def proj(g):
        q = dot(x, wqkv[:, g * 256:(g + 1) * 256]).astype(BF) * BF(0.125)
        k = dot(x, wqkv[:, 768 + g * 256:768 + (g + 1) * 256]).astype(BF)
        v = dot(x, wqkv[:, 1536 + g * 256:1536 + (g + 1) * 256]).astype(BF)
        return q, k, v
    nxt = proj(0)
    yield
    for g in range(3):
        q, k, v = nxt
        if g < 2:
            nxt = proj(g + 1)
            yield
        es = []
        for t in range(nt):
            sl = slice(t * SEQ, (t + 1) * SEQ)
            es.append(jnp.exp(dot_t(q[sl], bd(k[sl]))))
            if t % 2: yield
        e = jnp.concatenate(es, 0)
        p = (e / dot(e.astype(BF), ones_bd)).astype(BF)
        yield
        cs = []
        for t in range(nt):
            sl = slice(t * SEQ, (t + 1) * SEQ)
            cs.append(dot(p[sl], bd(v[sl])).astype(BF))
            if t % 2: yield
        ctx.append(jnp.concatenate(cs, 0))
    ctx = jnp.concatenate(ctx, 1)
    waits[1]()
    v = x.astype(F32) + dot(ctx, wout[...])
    yield
    out["normed"] = norm_rows(v).astype(BF)

def ff_steps(out, normed, wup, wdown, waits, fft=768):
    waits[0]()
    m = normed.shape[0]
    acc = normed.astype(F32)
    pre = dot(normed, wup[:, 0:fft])
    for j in range(0, 3072, fft):
        nxt = dot(normed, wup[:, j + fft:j + 2 * fft]) if j + fft < 3072 else None
        act = gelu(pre).astype(BF)
        pre = nxt
        if j == 0:
            waits[1]()
        acc = acc + dot(act, wdown[j:j + fft, :])
        yield
    hid = norm_rows(acc).astype(BF).astype(F32)
    pooled = jnp.mean(hid.reshape(m // SEQ, SEQ, 768), axis=1)
    out["emb"] = unit_rows(pooled)

def drain(gen):
    for _ in gen: pass

def mix(a, na, b, nb):
    da = db = 0
    la = lb = True
    while la or lb:
        if la and (not lb or da * nb <= db * na):
            try: next(a); da += 1
            except StopIteration: la = False
        elif lb:
            try: next(b); db += 1
            except StopIteration: lb = False

MESH = pl.DeviceIdType.MESH
INV_TEMP = 50.0


def pack(rows):
    return jnp.concatenate([rows[:, j * 128:(j + 1) * 128] for j in range(6)], axis=0)


def unpack(blocks):
    n = blocks.shape[0]
    parts = blocks.reshape(n, 6, 8, 128)
    return jnp.concatenate([parts[:, j].reshape(n * 8, 128) for j in range(6)], axis=1)


def to_row(col):
    n = col.shape[0]
    return jnp.transpose(jnp.broadcast_to(col, (n, 128)))[0:1, :]


def iota(shape, dim):
    return lax.broadcasted_iota(jnp.int32, shape, dim)


def hot(mask):
    return mask.astype(F32).astype(BF)


def step_kernel(
    x_hbm, qkv_h, out_h, up_h, down_h, queue_ref, qid_ref, pos_ref, tid_ref,
    loss_ref, qgrad_ref, tgrad_ref,
    wqkv, wout, wup, wdown, xs, keys, qids, ids, true_col, own_pack, mate_pack,
    gq, gt, queries, tails, ubuf, rbuf, qtot, tail_exp, tot_out, tot_in, grad_out, grad_in, tg_out, tg_in,
    w_sem, x_sem, agq_recv, agt_recv, ag_send, rs_send, rs_recv, tot_send, tot_recv, m_send, m_recv,
):
    tower, dp = lax.axis_index("tower"), lax.axis_index("dp")
    core, chip = lax.rem(dp, 2), lax.div(dp, 2)
    place = tower * 32 + chip
    mate = 1 - core
    mate_dev = (tower, chip * 2 + mate)
    handler = lax.rem(chip, 2) == core

    def same_core(n):
        return (lax.div(n, 32), lax.rem(n, 32) * 2 + core)

    def loop(first, last, body):
        def f(i, _):
            body(i)
            return 0
        lax.fori_loop(first, last, f, 0)

    barrier = pltpu.get_barrier_semaphore()
    loop(1, 64, lambda j: pl.semaphore_signal(barrier, inc=1, device_id=same_core(lax.rem(place + j, 64)), device_id_type=MESH))
    pl.semaphore_signal(barrier, inc=1, device_id=mate_dev, device_id_type=MESH)

    loads = [pltpu.make_async_copy(s.at[0, 0], d, w_sem.at[i]) for i, (s, d) in enumerate(
        [(qkv_h, wqkv), (out_h, wout), (up_h, wup), (down_h, wdown)])]
    x_loads = [pltpu.make_async_copy(x_hbm.at[h], xs.at[h], x_sem.at[h]) for h in range(2)]
    x_loads[0].start()
    loads[0].start()

    def remote(src, dst, ssem, rsem, dev):
        return pltpu.make_async_remote_copy(src_ref=src, dst_ref=dst, send_sem=ssem, recv_sem=rsem, device_id=dev, device_id_type=MESH)

    def key_rows(i):
        rows = pl.ds(pl.multiple_of(i * 128, 128), 128)
        keys[0, rows, :] = unit_rows(queue_ref[rows, :].astype(F32)).astype(BF)
    loop(0, 4, key_rows)
    qids[0] = qid_ref[...]
    pos = pos_ref[...]
    tid = tid_ref[...].astype(F32)
    true_row = jnp.zeros((1, 1024), F32)
    for j in range(0, 1024, 256):
        true_row = true_row + dot(jnp.broadcast_to(tid[:, j:j + 256], (16, 256)).astype(BF), hot(iota((256, 1024), 0) + j == pos))[0:1, :]
    pos_hi = lax.div(pos, 32)
    mixed = jnp.concatenate([jnp.broadcast_to(v, (8, 1024)) for v in (pos_hi.astype(F32), (pos - 32 * pos_hi).astype(F32), true_row, true_row)], axis=0).astype(BF)
    for h in range(2):
        p = iota((1024, 256), 1)
        source = (lax.div(p, 8) * 2 + core) * 16 + h * 8 + lax.rem(p, 8)
        got = dot(mixed, hot(iota((1024, 256), 0) == source))
        ids[0:1, h * 256:(h + 1) * 256] = got[0:1] * 32.0 + got[8:9]
        ids[1:2, h * 256:(h + 1) * 256] = got[16:17]
        true_col[h * 256:(h + 1) * 256, :] = jnp.transpose(jnp.broadcast_to(got[16:17], (128, 256)))

    def arrived(ref, sem):
        remote(ref, ref, m_send.at[0], sem, mate_dev).wait_recv()

    def left(ref, sem):
        remote(ref, ref, sem, m_recv.at[0], mate_dev).wait_send()

    def gather_wait(h, side, buf, sems):
        @pl.when(tower == side)
        def _():
            arrived(buf.at[pl.ds(0, 31)], sems.at[h])
        @pl.when(tower != side)
        def _():
            arrived(buf, sems.at[h])

    def to_all(h, dst, sems):
        def one(j):
            remote(own_pack.at[h], dst, ag_send.at[h], sems.at[h], same_core(lax.rem(place + HOP * j, 64))).start()
        loop(1, 64, one)

    def send_queries(h):
        @pl.when(tower == 0)
        def _():
            gq[h, chip] = own_pack[h]
            to_all(h, gq.at[h, chip], agq_recv)
        remote(own_pack.at[h], mate_pack.at[h], m_send.at[h], m_recv.at[h], mate_dev).start()

    def send_tails(h):
        @pl.when(tower == 1)
        def _():
            gt[h, core, chip] = own_pack[h]
            to_all(h, gt.at[h, core, chip], agt_recv)

    def queue_part(h):
        gather_wait(h, 0, gq.at[h], agq_recv)
        q = unpack(gq[h].astype(F32)).astype(BF)
        queries[pl.ds(h * 256, 256), :] = q
        total = jnp.zeros((256, 1), F32)
        u = jnp.zeros((256, 768), F32)
        truth = true_col[pl.ds(h * 256, 256), 0:1]
        for who in range(2):
            k = keys[who]
            s = INV_TEMP * dot_t(q, k)
            e = jnp.where(truth != qids[who].astype(F32), jnp.exp(s), 0.0)
            total = total + jnp.sum(e, axis=1, keepdims=True)
            u = u + dot(e.astype(BF), k)
        qtot[h] = to_row(total)
        for s in range(32):
            ubuf[h, s] = pack(u[s * 8:(s + 1) * 8]).astype(BF)
        def one(j):
            s = lax.rem(j * STRIDE + chip, 32)
            dest = lax.div(s, 16) * 32 + lax.rem(2 * s + core, 32)
            @pl.when(dest == place)
            def _():
                rbuf[h, place] = ubuf[h, s]
            @pl.when(dest != place)
            def _():
                remote(ubuf.at[h, s], rbuf.at[h, place], rs_send.at[h], rs_recv.at[h], same_core(dest)).start()
        loop(0, 32, one)

    keys_copy = remote(keys.at[0], keys.at[1], m_send.at[2], m_recv.at[2], mate_dev)
    qids_copy = remote(qids.at[0], qids.at[1], m_send.at[3], m_recv.at[3], mate_dev)

    def nothing():
        pass

    def half(h):
        out = {}
        x_loads[h].wait()
        for _ in att_steps(out, xs[h], wqkv, wout, (loads[0].wait, loads[1].wait) if h == 0 else (nothing, nothing)):
            pass
        if h == 0:
            pl.semaphore_wait(barrier, 64)
            keys_copy.start()
            qids_copy.start()
        elif not EARLY:
            send_tails(0)
        for i, _ in enumerate(ff_steps(out, out["normed"], wup, wdown, (loads[2].wait, loads[3].wait) if h == 0 else (nothing, nothing))):
            if h == 1 and i == MID:
                keys_copy.wait_recv()
                qids_copy.wait_recv()
                queue_part(0)
        own_pack[h] = pack(out["emb"]).astype(BF)
        send_queries(h)
        if h == 0 and EARLY or h == 1 and not LATE:
            send_tails(h)

    for c in loads[1:]:
        c.start()
    x_loads[1].start()
    half(0)
    half(1)
    if MID is None:
        keys_copy.wait_recv()
        qids_copy.wait_recv()
        queue_part(0)

    def forward_tails(h):
        gather_wait(h, 1, gt.at[h, core], agt_recv)
        remote(gt.at[h, core], gt.at[h, core], m_send.at[4 + h], m_recv.at[4 + h], mate_dev).start()

    def pack_wait(h):
        remote(mate_pack.at[h], mate_pack.at[h], m_send.at[h], m_recv.at[h], mate_dev).wait_recv()
    pack_wait(0)
    pack_wait(1)
    forward_tails(0)

    rows = iota((32, 1024), 0)
    lane = iota((32, 1024), 1)
    own = jnp.where(rows < 16, place * 16 + rows, dp * 16 + rows - 16)
    sel = lane == own
    own_pos = jnp.sum(jnp.where(sel, pos.astype(F32), 0.0), axis=1, keepdims=True).astype(jnp.int32)
    own_true = jnp.sum(jnp.where(sel, true_row, 0.0), axis=1, keepdims=True)
    at_pos = hot(lane == own_pos)
    skip = (lane == own_pos) | (tid == own_true)

    queue_part(1)
    if LATE == 1:
        send_tails(1)

    pos_q, true_q = ids[0:1, :].astype(jnp.int32), ids[1:2, :]
    row = iota((32, 512), 0)
    is_pos = pos_q == chip * 32 + row
    chip_ids = jnp.sum(jnp.where(iota((32, 1024), 1) == chip * 32 + iota((32, 1024), 0), tid, 0.0), axis=1, keepdims=True)

    def tail_scores(mine, other):
        mine, other = unpack(mine), unpack(other)
        first = jnp.where(core == 0, mine, other)
        second = jnp.where(core == 0, other, mine)
        t32 = jnp.concatenate([first, second], axis=0).astype(BF)
        s = INV_TEMP * dot_t(t32, queries[...]) - is_pos.astype(F32)
        tail_exp[...] = jnp.where(is_pos | (chip_ids != true_q), jnp.exp(s), 0.0)

    total = jnp.concatenate([qtot[0], qtot[1]], axis=1)
    @pl.when(tower == 1)
    def _():
        tail_scores(own_pack[...].astype(F32), mate_pack[...].astype(F32))
    tail_part = jnp.sum(tail_exp[...], axis=0, keepdims=True)
    tot_out[...] = total + jnp.where(tower == 1, tail_part, 0.0)
    tot_in[place] = tot_out[...]
    loop(1, 64, lambda j: remote(tot_out, tot_in.at[place], tot_send.at[0], tot_recv.at[0], same_core(lax.rem(place + HOP * j, 64))).start())

    if LATE == 2:
        send_tails(1)

    forward_tails(1)
    for h in range(2):
        remote(gt.at[h, mate], gt.at[h, mate], m_send.at[4 + h], m_recv.at[4 + h], mate_dev).wait_recv()
    @pl.when(tower == 0)
    def _():
        tail_scores(gt[:, core, chip].astype(F32), gt[:, mate, chip].astype(F32))
    for who in range(2):
        halves = [unpack(gt[h, who].astype(F32)).reshape(32, 8, 768) for h in range(2)]
        tails[:, who] = jnp.concatenate(halves, axis=1).astype(BF)
    all_tails = tails[...].reshape(1024, 768)

    def query_rows(d):
        return jnp.concatenate([unpack(gq[h, pl.ds(lax.div(d, 2), 1)].astype(F32)) for h in range(2)], axis=0)
    own_q = jnp.concatenate([query_rows(place), query_rows(dp)], axis=0)
    own_s = INV_TEMP * dot_t(own_q[:16].astype(BF), all_tails)
    own_e = jnp.where(skip[:16], 0.0, jnp.exp(own_s))
    taken = dot(jnp.concatenate([own_e.astype(BF), at_pos], axis=0), all_tails)
    from_tails, pos_emb = taken[:16], taken[16:]
    logit = INV_TEMP * jnp.sum(own_q * pos_emb, axis=1, keepdims=True) - 1.0

    for h in range(2):
        left(rbuf.at[h, pl.ds(0, 63)], ag_send.at[h])
        @pl.when(handler)
        def _():
            left(ubuf.at[h, pl.ds(0, 31)], rs_send.at[h])
        @pl.when(jnp.logical_not(handler))
        def _():
            left(ubuf.at[h], rs_send.at[h])
        left(mate_pack.at[h], m_send.at[h])
        left(gt.at[h, core], m_send.at[4 + h])
    keys_copy.wait_send()
    qids_copy.wait_send()
    left(tot_in.at[pl.ds(0, 63)], tot_send.at[0])

    arrived(tot_in.at[pl.ds(0, 63)], tot_recv.at[0])
    total = jnp.sum(tot_in[...], axis=0)

    weights = (tail_exp[...] / total - is_pos.astype(F32)).astype(BF)
    tg_out[...] = (INV_TEMP * dot(weights, queries[...])).reshape(2, 16, 768)
    tg_copy = remote(tg_out.at[mate], tg_in, m_send.at[6], m_recv.at[6], mate_dev)
    tg_copy.start()

    p = iota((32, 512), 1)
    place_of = (lax.div(lax.rem(p, 256), 8) * 2 + core) * 16 + lax.div(p, 256) * 8 + lax.rem(p, 8)
    own512 = jnp.where(iota((32, 512), 0) < 16, place * 16 + iota((32, 512), 0), dp * 16 + iota((32, 512), 0) - 16)
    own_total = jnp.sum(jnp.where(place_of == own512, total, 0.0), axis=1, keepdims=True)
    loss = jnp.log(own_total[16:]) - logit[16:]
    loss_ref[...] = jnp.sum(jnp.where(iota((16, 16), 0) == iota((16, 16), 1), loss, 0.0), axis=0, keepdims=True)

    grad_copy = remote(grad_out, grad_in, m_send.at[7], m_recv.at[7], mate_dev)
    @pl.when(handler)
    def _():
        def summed(h):
            arrived(rbuf.at[h, pl.ds(0, 63)], rs_recv.at[h])
            def add(s, acc):
                for i in range(4):
                    acc = acc + rbuf[h, s * 4 + i].astype(F32)
                return acc
            return lax.fori_loop(0, 16, add, jnp.zeros((48, 128), F32))
        u = unpack(jnp.stack([summed(0), summed(1)]))
        excess = jnp.exp(logit[:16]) / own_total[:16] - 1.0
        grad = INV_TEMP * ((u + from_tails) / own_total[:16] + excess * pos_emb[:16])
        grad_out[...] = jnp.where(core == 0, grad[8:], grad[:8])
        grad_copy.start()
        qgrad_ref[...] = jnp.where(core == 0, grad[:8], grad[8:])
    @pl.when(jnp.logical_not(handler))
    def _():
        grad_copy.wait_recv()
        qgrad_ref[...] = grad_in[...]
    tg_copy.wait_recv()
    tgrad_ref[...] = jnp.where(core == 0, tg_out[0], tg_out[1]) + tg_in[...]

    @pl.when(handler)
    def _():
        grad_copy.wait_send()
    tg_copy.wait_send()


MID = 2
STRIDE = 5
HOP = 21
LATE = 0
VM = 60
EARLY = False


def local(token_states, qkv_weight, out_weight, up_weight, down_weight, queue_states, queue_ids, positive, tail_ids):
    vm, anywhere = pl.BlockSpec(memory_space=pltpu.VMEM), pl.BlockSpec(memory_space=pl.ANY)
    dma = pltpu.SemaphoreType.DMA
    loss, qgrad, tgrad = pl.pallas_call(
        step_kernel,
        out_shape=(
            jax.ShapeDtypeStruct((1, 16), F32),
            jax.ShapeDtypeStruct((8, 768), F32),
            jax.ShapeDtypeStruct((16, 768), F32),
        ),
        in_specs=[anywhere] * 5 + [vm] * 4,
        out_specs=(vm, vm, vm),
        scratch_shapes=[
            pltpu.VMEM((768, 2304), BF), pltpu.VMEM((768, 768), BF), pltpu.VMEM((768, 3072), BF), pltpu.VMEM((3072, 768), BF),
            pltpu.VMEM((2, 512, 768), BF),
            pltpu.VMEM((2, 512, 768), BF),
            pltpu.VMEM((2, 1, 512), jnp.int32),
            pltpu.VMEM((8, 512), F32),
            pltpu.VMEM((512, 128), F32),
            pltpu.VMEM((2, 48, 128), BF),
            pltpu.VMEM((2, 48, 128), BF),
            pltpu.VMEM((2, 32, 48, 128), BF),
            pltpu.VMEM((2, 2, 32, 48, 128), BF),
            pltpu.VMEM((512, 768), BF),
            pltpu.VMEM((32, 2, 16, 768), BF),
            pltpu.VMEM((2, 32, 48, 128), BF),
            pltpu.VMEM((2, 64, 48, 128), BF),
            pltpu.VMEM((2, 1, 256), F32),
            pltpu.VMEM((32, 512), F32),
            pltpu.VMEM((1, 512), F32),
            pltpu.VMEM((64, 1, 512), F32),
            pltpu.VMEM((8, 768), F32),
            pltpu.VMEM((8, 768), F32),
            pltpu.VMEM((2, 16, 768), F32),
            pltpu.VMEM((16, 768), F32),
            dma((4,)), dma((2,)), dma((2,)), dma((2,)), dma((2,)), dma((2,)), dma((2,)),
            dma((1,)), dma((1,)), dma((8,)), dma((8,)),
        ],
        compiler_params=pltpu.CompilerParams(
            collective_id=0, has_side_effects=True, vmem_limit_bytes=VM * 2**20
        ),
    )(token_states.reshape(2, 512, 768), qkv_weight, out_weight, up_weight, down_weight,
      queue_states, queue_ids.reshape(1, 512), positive.reshape(1, 1024), tail_ids.reshape(1, 1024))
    def finish(*refs):
        for src, dst in zip(refs[:3], refs[3:]):
            dst[...] = src[...]
    loss, qgrad, tgrad = pl.pallas_call(
        finish,
        out_shape=tuple(jax.ShapeDtypeStruct(v.shape, F32) for v in (loss, qgrad, tgrad)),
        in_specs=[vm] * 3,
        out_specs=(vm, vm, vm),
    )(loss, qgrad, tgrad)
    return loss.reshape(16), qgrad, tgrad


def solution(mesh):
    placed = (
        P("tower", "dp", None, None),
        P("tower", None, None, None),
        P("tower", None, None, None),
        P("tower", None, None, None),
        P("tower", None, None, None),
        P(("tower", "dp"), None),
        P(("tower", "dp")),
        P(),
        P(),
    )
    return jax.shard_map(
        local,
        mesh=mesh,
        in_specs=placed,
        out_specs=(P("dp"), P(("tower", "dp"), None), P("dp", None)),
        check_vma=False,
    )
```
